128 devices in a mesh: gx: 16 (over z, y), gy: 8 (over x, core).
Axes of the slice: x: 4, y: 4, z: 4, core: 2. Of those that a mesh axis runs over, the one named last changes fastest.
Arguments:
- ensemble: bfloat16 [2, 3, 128, 512, 1024], P(None, None, None, 'gx', 'gy'), may hold values from -6 to 6
- layer_depth: float32 [2, 512, 1024], P(None, 'gx', 'gy'), may hold values from 0.5 to 2
- obs_dest: int32 [16, 8, 32], P('gx', 'gy'), may hold values from 0 to 7, as said below
- obs_cell: int32 [16, 8, 32, 128], P('gx', 'gy'), may hold values from 0 to 4095
- obs_value: float32 [16, 8, 32, 128], P('gx', 'gy'), may hold values from -10 to 10
- obs_sigma: float32 [16, 8, 32, 128], P('gx', 'gy'), may hold values from 2 to 20
Outputs:
- analysis: bfloat16 [2, 3, 128, 512, 1024], P(None, None, None, 'gx', 'gy')
The draws below stay inside these ranges and needn't reach their ends.
Inputs may be any that keep to these rules, and one draw needn't show every extreme that they name: `obs_dest`: at most 10 blocks of one tile name one tile column, and in every row of tiles one column is named by exactly 10 blocks of every tile of that row. `obs_cell`: cells are numbered row by row, 128 to a row.
All inputs are finite; a program needn't handle non-finite values.
Results may differ from the reference program's by a relative error of at most 0.025.
Values may be sent and summed in bfloat16 or wider, within the bound.
No kernel may reach another device: no remote copies, remote signals or barrier semaphores. Data moves between devices by JAX's collectives and lax.ppermute only.
A program may use at most 128 MiB of HBM per device.

```python
import math
import jax
import jax.numpy as jnp
from jax import lax

ENSEMBLE_SIZE = 128
OBS = 128
PATCH_LATITUDES = 32
TY = 128
STEPS = 4
BLK = 32
CAP = 10
TILES_X = 16
TILES_Y = 8
NX = 512
NY = 1024


def smooth_field(key, amplitude):
    key_kx, key_ky, key_phase = jax.random.split(key, 3)
    wave_x = jax.random.randint(key_kx, (2,), 1, 4).astype(jnp.float32)
    wave_y = jax.random.randint(key_ky, (2,), 1, 4).astype(jnp.float32)
    phase = jax.random.uniform(key_phase, (2,), jnp.float32, -3.14159, 3.14159)
    grid_x = lax_rows()
    grid_y = lax_cols()
    angle_one = 6.2831853 * (wave_x[0] * grid_x + wave_y[0] * grid_y) + phase[0]
    angle_two = 6.2831853 * (wave_x[1] * grid_x + wave_y[1] * grid_y) + phase[1]
    return jnp.stack([amplitude * jnp.cos(angle_one), amplitude * jnp.cos(angle_two)])


def lax_rows():
    return (jnp.arange(NX, dtype=jnp.int32).astype(jnp.float32) / NX)[:, None]


def lax_cols():
    return (jnp.arange(NY, dtype=jnp.int32).astype(jnp.float32) / NY)[None, :]


def member_mode(key, amplitude):
    key_field, key_coef = jax.random.split(key, 2)
    fields = smooth_field(key_field, amplitude)
    coefs = jnp.clip(jax.random.normal(key_coef, (ENSEMBLE_SIZE,), jnp.float32), -2.5, 2.5)
    return fields[:, None, :, :] * coefs[None, :, None, None]


def draw_ensemble(key, part):
    key = jax.random.fold_in(key, 11)
    key_noise, key_first = jax.random.split(key, 2)
    shape = (2, 3, ENSEMBLE_SIZE, NX, NY)
    noise = jax.random.truncated_normal(key_noise, -6.0, 6.0, shape, jnp.float32)
    mode = member_mode(key_first, 1.4)
    is_thick = (jnp.arange(3, dtype=jnp.int32) == 2).astype(jnp.float32)[None, :, None, None, None]
    total = noise + is_thick * mode[:, None]
    return jnp.clip(total, -6.0, 6.0).astype(jnp.bfloat16)


def draw_obs_dest(key, part):
    key = jax.random.fold_in(key, 5)
    key_hot, key_pool, key_order = jax.random.split(key, 3)
    tiles = TILES_X * TILES_Y
    hot = jax.random.randint(key_hot, (TILES_X,), 0, TILES_Y)
    hot_each = jnp.repeat(hot, TILES_Y)
    pool_keys = jax.random.split(key_pool, tiles)

    def pool_draw(inner_key):
        return jax.random.permutation(inner_key, (TILES_Y - 1) * CAP)
    drawn = jax.vmap(pool_draw)(pool_keys)
    others = drawn[:, :BLK - CAP] // CAP
    others = others + (others >= hot_each[:, None]).astype(jnp.int32)
    hot_cols = jnp.broadcast_to(hot_each[:, None], (tiles, CAP))
    blocks = jnp.concatenate([hot_cols, others], 1).astype(jnp.int32)
    order_keys = jax.random.split(key_order, tiles)

    def order_draw(inner_key):
        return jax.random.permutation(inner_key, BLK)
    orders = jax.vmap(order_draw)(order_keys)
    blocks = jnp.take_along_axis(blocks, orders, 1)
    return blocks.reshape(TILES_X, TILES_Y, BLK)


def with_ends(values, stream_key, least, high):
    spot = [jax.random.randint(jax.random.fold_in(stream_key, axis), (), 0, length) for axis, length in enumerate(values.shape)]
    widest = values.shape.index(max(values.shape))
    next_to = spot[:widest] + [(spot[widest] + 1) % values.shape[widest]] + spot[widest + 1:]
    return values.at[tuple(spot)].set(least).at[tuple(next_to)].set(high)


def shard_levels(own_key, shape, shards, least, largest):
    def one(position, blocks):
        draws = jax.random.uniform(jax.random.fold_in(jax.random.fold_in(own_key, 6), position), (blocks,), jnp.float32, least / len(shards), largest / len(shards))
        return jnp.repeat(jnp.exp(draws), shape[position] // blocks).reshape((-1,) + (1,) * (len(shape) - position - 1))

    factor_of = one(*shards[0])
    for cut in shards[1:]:
        factor_of = factor_of * one(*cut)
    return factor_of


def normal_values(key, dims, deviation, limit, cuts=(), kind=jnp.bfloat16):
    loudness = shard_levels(key, dims, cuts, -0.22, 0.18) if cuts else 1.0
    entries = jax.random.normal(key, dims, jnp.float32) * deviation * loudness
    return jnp.minimum(jnp.maximum(entries, -limit), limit).astype(kind)


def setup_inputs(seed: int = 0) -> dict:
    seeds = jax.random.split(jax.random.key(seed), 7)
    return {
        "ensemble": draw_ensemble(jax.random.fold_in(seeds[6], 71), 0),
        "layer_depth": jnp.clip(0.5 + 1.5 * jax.random.uniform(seeds[1], (2, NX, NY), jnp.float32) ** shard_levels(seeds[1], (2, NX, NY), ((1, 16), (2, 8)), -0.2, 0.2), 0.5, 2.0),
        "obs_dest": draw_obs_dest(jax.random.fold_in(seeds[6], 71), 0),
        "obs_cell": with_ends(jax.random.randint(seeds[3], (TILES_X, TILES_Y, BLK, OBS), 0, PATCH_LATITUDES * TY), jax.random.fold_in(seeds[3], 1), 0, (PATCH_LATITUDES * TY) - 1).astype(jnp.int32),
        "obs_value": normal_values(seeds[4], (TILES_X, TILES_Y, BLK, OBS), 2.0, 10.0, ((0, 16), (1, 8)), jnp.float32),
        "obs_sigma": jnp.clip(jnp.exp(math.log(20.0) - 2.3025851 * jax.random.uniform(seeds[5], (TILES_X, TILES_Y, BLK, OBS), jnp.float32) ** shard_levels(seeds[5], (TILES_X, TILES_Y, BLK, OBS), ((0, 16), (1, 8)), -0.2, 0.2)), 2.0, 20.0),
    }


cfl_number = 0.3
coriolis = 0.4
coupling = 0.5

def diff_rows(field):
    padded = jnp.pad(field.astype(jnp.float32), ((0, 0), (1, 1), (0, 0)))
    return padded[:, 2:] - padded[:, :-2]

def diff_cols(field):
    padded = jnp.pad(field.astype(jnp.float32), ((0, 0), (0, 0), (1, 1)))
    return padded[:, :, 2:] - padded[:, :, :-2]

def advance(state, layer_depth):
    half_step = 0.5 * cfl_number
    vel_x = state[:, 0].astype(jnp.float32)
    vel_y = state[:, 1].astype(jnp.float32)
    thick = state[:, 2].astype(jnp.float32)
    flux_x = (layer_depth * vel_x).astype(jnp.bfloat16)
    flux_y = (layer_depth * vel_y).astype(jnp.bfloat16)
    spread_div = diff_rows(flux_x) + diff_cols(flux_y)
    thick_new = (thick - half_step * spread_div).astype(jnp.bfloat16)
    thick_f = thick_new.astype(jnp.float32)
    pressure = jnp.stack([thick_f[0] + thick_f[1], coupling * thick_f[0] + thick_f[1]]).astype(jnp.bfloat16)
    grad_x = diff_rows(pressure)
    grad_y = diff_cols(pressure)
    turn = cfl_number * coriolis
    vel_x_new = (vel_x + turn * vel_y - half_step * grad_x).astype(jnp.bfloat16)
    vel_y_new = (vel_y - turn * vel_x - half_step * grad_y).astype(jnp.bfloat16)
    return jnp.stack([vel_x_new, vel_y_new, thick_new], 1)

def make_transform(gram, proj, members):
    eye = jnp.eye(members, dtype=jnp.float32)
    lower = jnp.linalg.cholesky(gram)
    inverse = lax.linalg.triangular_solve(lower, eye, left_side=True, lower=True)
    inner = jnp.dot(inverse.astype(jnp.float32), proj.astype(jnp.float32), precision=lax.Precision.HIGHEST, preferred_element_type=jnp.float32)
    weights = jnp.dot(inverse.T.astype(jnp.float32), inner.astype(jnp.float32), precision=lax.Precision.HIGHEST, preferred_element_type=jnp.float32)
    scale = jnp.sqrt(jnp.float32(members - 1))
    return (weights[:, None] + scale * inverse.T).astype(jnp.bfloat16)

def reference(ensemble, layer_depth, obs_dest, obs_cell, obs_value, obs_sigma):

    def propagate_sample(member):
        state = lax.dynamic_index_in_dim(ensemble, member, 2, keepdims=False)
        for _ in range(STEPS):
            state = advance(state, layer_depth)
        surface_elevation = state[0, 2].astype(jnp.float32) + state[1, 2].astype(jnp.float32)
        return (state, surface_elevation)
    prior_state_array, surface_elevation = lax.map(propagate_sample, jnp.arange(ENSEMBLE_SIZE, dtype=jnp.int32))

    def accumulate(carry, patch_latitude_index):
        gram, proj = carry
        dest = obs_dest[patch_latitude_index]
        cells = obs_cell[patch_latitude_index]
        rows = patch_latitude_index * PATCH_LATITUDES + cells // TY
        cols = dest[:, :, None] * TY + cells % TY
        seen = surface_elevation[:, rows, cols]
        mean_seen = lax.optimization_barrier(jnp.mean(seen, 0))
        inv_sigma = 1.0 / obs_sigma[patch_latitude_index]
        spread = (seen - mean_seen) * inv_sigma
        innovation = (obs_value[patch_latitude_index] - mean_seen) * inv_sigma
        gram = gram + jnp.einsum('mybo,nybo->mn', spread, spread, precision=lax.Precision.HIGHEST)
        proj = proj + jnp.einsum('mybo,ybo->m', spread, innovation, precision=lax.Precision.HIGHEST)
        return ((gram, proj), None)
    start = (jnp.zeros((ENSEMBLE_SIZE, ENSEMBLE_SIZE), jnp.float32), jnp.zeros((ENSEMBLE_SIZE,), jnp.float32))
    (gram, proj), _ = lax.scan(accumulate, start, jnp.arange(TILES_X, dtype=jnp.int32))
    gram = gram + (ENSEMBLE_SIZE - 1) * jnp.eye(ENSEMBLE_SIZE, dtype=jnp.float32)
    transform = make_transform(gram, proj, ENSEMBLE_SIZE).astype(jnp.float32)

    def analyse(patch_latitude_index):
        patch_portion = lax.dynamic_slice_in_dim(prior_state_array, patch_latitude_index * PATCH_LATITUDES, PATCH_LATITUDES, 3)
        center = lax.optimization_barrier(jnp.mean(patch_portion.astype(jnp.float32), 0))
        anomaly = (patch_portion.astype(jnp.float32) - center).astype(jnp.bfloat16).astype(jnp.float32)
        mixed = jnp.einsum('nm,nlcxy->mlcxy', transform, anomaly, precision=lax.Precision.HIGHEST)
        return (center + mixed).astype(jnp.bfloat16)
    blocks = lax.map(analyse, jnp.arange(TILES_X, dtype=jnp.int32))
    result = jnp.transpose(blocks, (2, 3, 1, 0, 4, 5))
    return result.reshape(2, 3, ENSEMBLE_SIZE, NX, NY)
```

```python
import jax
import jax.numpy as jnp
from jax import lax
from jax.experimental import pallas as pl
from jax.experimental.pallas import tpu as pltpu
from jax.sharding import PartitionSpec as P

MEMBERS = 128
ROWS = 32
COLS = 128
HALO = 8
STEPS = 4
CHUNK = 32
CHUNKS = COLS // CHUNK
WIDE_ROWS = ROWS + 2 * HALO
WIDE_COLS = CHUNK + 2 * HALO
LAYERS = 2
HALF = 0.15
TURN = 0.12
COUPLING = 0.5
VMEM = 60 * 1024 * 1024

F32 = jnp.float32
BF16 = jnp.bfloat16


def params():
    return pltpu.CompilerParams(vmem_limit_bytes=VMEM)


def shift(x, axis, by):
    n = lax.axis_size(axis)
    return lax.ppermute(x, axis, [(i, (i + by) % n) for i in range(n)])


def to_lanes_kernel(e_ref, o_ref, rows):
    rows[...] = e_ref[0, 0].astype(F32).reshape(MEMBERS * ROWS, COLS)

    def body(x, carry):
        plane = rows[pl.ds(x, MEMBERS, stride=ROWS), :]
        o_ref[0, 0, x] = plane.T.astype(BF16)
        return carry

    lax.fori_loop(0, ROWS, body, 0, unroll=4)


def to_lanes(ensemble):
    return pl.pallas_call(
        to_lanes_kernel,
        grid=(LAYERS, 3),
        in_specs=[pl.BlockSpec((1, 1, MEMBERS, ROWS, COLS), lambda i, j: (i, j, 0, 0, 0))],
        out_specs=pl.BlockSpec((1, 1, ROWS, COLS, MEMBERS), lambda i, j: (i, j, 0, 0, 0)),
        out_shape=jax.ShapeDtypeStruct((LAYERS, 3, ROWS, COLS, MEMBERS), BF16),
        scratch_shapes=[pltpu.VMEM((MEMBERS * ROWS, COLS), F32)],
        compiler_params=params(),
        name="to_lanes",
    )(ensemble)


def forecast_kernel(
    chunk, et, sides, top, bottom, corner_t, corner_b, depth, col_scale, row_scale,
    out, raw, raw_side, dep, us, vs, hs, fx, fy, pr, sems,
):
    first, last = chunk == 0, chunk == CHUNKS - 1
    lo = 0 if first else chunk * CHUNK - 16
    hi = COLS if last else chunk * CHUNK + 48
    at = 16 if first else 0
    src, dst = pl.ds(lo, hi - lo), pl.ds(at, hi - lo)
    parts = [
        (et.at[:, :, :, src], raw.at[:, :, HALO:HALO + ROWS, dst]),
        (top.at[:, :, :, src], raw.at[:, :, 0:HALO, dst]),
        (bottom.at[:, :, :, src], raw.at[:, :, HALO + ROWS:WIDE_ROWS, dst]),
        (depth.at[:, :, pl.ds(chunk * CHUNK, WIDE_COLS)], dep),
    ]
    if first or last:
        parts += [
            (sides, raw_side.at[:, :, HALO:HALO + ROWS]),
            (corner_t, raw_side.at[:, :, 0:HALO]),
            (corner_b, raw_side.at[:, :, HALO + ROWS:WIDE_ROWS]),
        ]
    copies = [pltpu.make_async_copy(a, b, sems.at[k]) for k, (a, b) in enumerate(parts)]
    for c in copies:
        c.start()
    for c in copies:
        c.wait()

    def load(l, c, r):
        x = raw[l, c, r].astype(F32)
        if first:
            return jnp.concatenate([raw_side[l, c, r].astype(F32)[0:8], x[16:56]], axis=0)
        if last:
            return jnp.concatenate([x[8:48], raw_side[l, c, r].astype(F32)[8:16]], axis=0)
        return x[8:56]

    mid = pl.ds(8, WIDE_COLS)
    left, right = pl.ds(7, WIDE_COLS), pl.ds(9, WIDE_COLS)

    def unpack(r, carry):
        for l in range(LAYERS):
            d = dep[l, r]
            u, v = load(l, 0, r), load(l, 1, r)
            us[l, r] = u
            vs[l, r] = v
            hs[l, r] = load(l, 2, r)
            fx[l, r] = d * u
            fy[l, r, mid] = d * v
        return carry

    lax.fori_loop(0, WIDE_ROWS, unpack, 0)
    cs = col_scale[pl.ds(chunk * CHUNK, WIDE_COLS), :]
    inner = slice(HALO, HALO + CHUNK)

    for step in range(1, STEPS + 1):
        final = step == STEPS

        def thickness(r, carry):
            new = []
            for l in range(LAYERS):
                div = (fx[l, r + 1] - fx[l, r - 1]) + (fy[l, r, right] - fy[l, r, left])
                h = hs[l, r] - div
                hs[l, r] = h
                new.append(h)
            scale = cs * row_scale[0, r]
            pr[0, r, mid] = (new[0] + new[1]) * scale
            pr[1, r, mid] = (COUPLING * new[0] + new[1]) * scale
            return carry

        lax.fori_loop(2 * step - 1, WIDE_ROWS - (2 * step - 1), thickness, 0)

        def velocity(r, carry):
            for l in range(LAYERS):
                u, v = us[l, r], vs[l, r]
                u_new = (u + TURN * v) - (pr[l, r + 1, mid] - pr[l, r - 1, mid])
                v_new = (v - TURN * u) - (pr[l, r, right] - pr[l, r, left])
                if final:
                    out[l, 0, r - HALO] = u_new[inner].astype(BF16)
                    out[l, 1, r - HALO] = v_new[inner].astype(BF16)
                    out[l, 2, r - HALO] = hs[l, r, inner].astype(BF16)
                else:
                    d = dep[l, r]
                    us[l, r] = u_new
                    vs[l, r] = v_new
                    fx[l, r] = d * u_new
                    fy[l, r, mid] = d * v_new
            return carry

        lax.fori_loop(2 * step, WIDE_ROWS - 2 * step, velocity, 0)


def forecast(chunk, et, sides, top, bottom, corner_t, corner_b, depth, col_scale, row_scale):
    plane = (LAYERS, WIDE_ROWS, WIDE_COLS, MEMBERS)
    padded = (LAYERS, WIDE_ROWS, WIDE_COLS + 16, MEMBERS)
    anywhere = pl.BlockSpec(memory_space=pl.ANY)

    def kernel(*refs):
        forecast_kernel(chunk, *refs)

    return pl.pallas_call(
        kernel,
        in_specs=[anywhere] * 7
        + [pl.BlockSpec(memory_space=pltpu.VMEM), pl.BlockSpec(memory_space=pltpu.SMEM)],
        out_specs=pl.BlockSpec(memory_space=pltpu.VMEM),
        out_shape=jax.ShapeDtypeStruct((LAYERS, 3, ROWS, CHUNK, MEMBERS), BF16),
        scratch_shapes=[
            pltpu.VMEM((LAYERS, 3, WIDE_ROWS, 64, MEMBERS), BF16),
            pltpu.VMEM((LAYERS, 3, WIDE_ROWS, 16, MEMBERS), BF16),
            pltpu.VMEM(plane, F32),
            pltpu.VMEM(plane, F32),
            pltpu.VMEM(plane, F32),
            pltpu.VMEM(plane, F32),
            pltpu.VMEM(plane, F32),
            pltpu.VMEM(padded, F32),
            pltpu.VMEM(padded, F32),
            pltpu.SemaphoreType.DMA((7,)),
        ],
        compiler_params=params(),
        name="forecast_%d" % chunk,
    )(et, sides, top, bottom, corner_t, corner_b, depth, col_scale, row_scale)


def gram_kernel(s0, s1, s2, s3, weight, pull, out, high, low):
    def body(x, acc):
        for j, s in enumerate((s0, s1, s2, s3)):
            cols = slice(j * CHUNK, (j + 1) * CHUNK)
            ssh = s[0, 0, x].astype(F32) + s[1, 0, x].astype(F32)
            mean = jnp.sum(ssh, axis=1, keepdims=True) * (1.0 / MEMBERS)
            z = ssh - mean
            w = weight[x, cols]
            y = z * jnp.sqrt(w)
            y_high = y.astype(BF16)
            at = pl.ds(pl.multiple_of(x * COLS + j * CHUNK, CHUNK), CHUNK)
            high[at, :] = y_high
            low[at, :] = (y - y_high.astype(F32)).astype(BF16)
            acc = acc + z * (pull[x, cols] - mean * w)
        return acc

    acc = lax.fori_loop(0, ROWS, body, jnp.zeros((CHUNK, MEMBERS), F32))
    contract = (((0,), (0,)), ((), ()))
    main = lax.dot_general(high[...], high[...], contract, preferred_element_type=F32)
    cross = lax.dot_general(high[...], low[...], contract, preferred_element_type=F32)
    out[0:MEMBERS, :] = main + (cross + cross.T)
    out[MEMBERS:MEMBERS + 8, :] = jnp.broadcast_to(
        jnp.sum(acc, axis=0, keepdims=True), (8, MEMBERS)
    )


def gram_of(states, weight, pull):
    heights = pl.BlockSpec((LAYERS, 1, ROWS, CHUNK, MEMBERS), lambda i: (0, 2, 0, 0, 0))
    cells = pl.BlockSpec((ROWS, COLS, MEMBERS), lambda i: (0, 0, 0))
    return pl.pallas_call(
        gram_kernel,
        grid=(1,),
        in_specs=[heights] * CHUNKS + [cells, cells],
        out_specs=pl.BlockSpec((MEMBERS + 8, MEMBERS), lambda i: (0, 0)),
        out_shape=jax.ShapeDtypeStruct((MEMBERS + 8, MEMBERS), F32),
        scratch_shapes=[
            pltpu.VMEM((ROWS * COLS, MEMBERS), BF16),
            pltpu.VMEM((ROWS * COLS, MEMBERS), BF16),
        ],
        compiler_params=params(),
        name="gram",
    )(*states, weight, pull)


def analysis_kernel(s0, s1, s2, s3, transform_t, out, rows):
    share = jnp.full((MEMBERS, MEMBERS), 1.0 / MEMBERS, BF16)
    share_row = jnp.full((8, MEMBERS), 1.0 / MEMBERS, BF16)
    over_last = (((1,), (1,)), ((), ()))
    tt = transform_t[...]

    def body(x, carry):
        s = jnp.concatenate([r[0, 0, x] for r in (s0, s1, s2, s3)], axis=0)
        center = jnp.dot(s, share, preferred_element_type=F32)
        anomaly = (s.astype(F32) - center).astype(BF16)
        center_row = lax.dot_general(share_row, s, over_last, preferred_element_type=F32)
        mixed = lax.dot_general(tt, anomaly, over_last, preferred_element_type=F32)
        rows[pl.ds(x, MEMBERS, stride=ROWS), :] = mixed + center_row[0:1]
        return carry

    lax.fori_loop(0, ROWS, body, 0, unroll=2)
    out[0, 0] = rows[...].reshape(MEMBERS, ROWS, COLS).astype(BF16)


def analyse(states, transform_t):
    part = pl.BlockSpec((1, 1, ROWS, CHUNK, MEMBERS), lambda i, j: (i, j, 0, 0, 0))
    return pl.pallas_call(
        analysis_kernel,
        grid=(LAYERS, 3),
        in_specs=[part] * CHUNKS + [pl.BlockSpec((MEMBERS, MEMBERS), lambda i, j: (0, 0))],
        out_specs=pl.BlockSpec((1, 1, MEMBERS, ROWS, COLS), lambda i, j: (i, j, 0, 0, 0)),
        out_shape=jax.ShapeDtypeStruct((LAYERS, 3, MEMBERS, ROWS, COLS), BF16),
        scratch_shapes=[pltpu.VMEM((MEMBERS * ROWS, COLS), F32)],
        compiler_params=params(),
        name="analysis",
    )(*states, transform_t)


def split3(x):
    a = lax.reduce_precision(x, 8, 7)
    b = lax.reduce_precision(x - a, 8, 7)
    c = lax.reduce_precision(x - a - b, 8, 7)
    return [p.astype(BF16) for p in (a, b, c)]


def observed_cells(dest, cell, value, sigma):
    tiles = lax.axis_size("gy")
    inverse = 1.0 / sigma
    weight = inverse * inverse
    pieces = jnp.stack(split3(weight) + split3(value * weight), 0).reshape(6, -1)
    row = (dest[:, None] * ROWS + cell // COLS).reshape(-1)
    col = (cell % COLS).reshape(-1)
    row_hot = (row[None, :] == jnp.arange(tiles * ROWS, dtype=jnp.int32)[:, None]).astype(BF16)
    col_hot = col[:, None] == jnp.arange(COLS, dtype=jnp.int32)[None, :]
    spread = jnp.where(col_hot[None], pieces[:, :, None], jnp.zeros((), BF16))
    field = jnp.einsum("rk,pkc->prc", row_hot, spread, preferred_element_type=F32)
    field = jnp.stack([field[2] + field[1] + field[0], field[5] + field[4] + field[3]], 0)
    field = field.reshape(2, tiles, ROWS, COLS).transpose(1, 0, 2, 3)
    me = lax.axis_index("gy")
    bit = tiles // 2
    while bit:
        pair = field.reshape((2, bit) + field.shape[1:])
        mine = (me // bit) % 2
        keep = lax.dynamic_index_in_dim(pair, mine, 0, keepdims=False)
        send = lax.dynamic_index_in_dim(pair, 1 - mine, 0, keepdims=False)
        field = keep + lax.ppermute(send, "gy", [(i, i ^ bit) for i in range(tiles)])
        bit //= 2
    return field[0, 0], field[0, 1]


def sum_everywhere(x):
    def other(axis, k):
        return lax.ppermute(x, axis, [(i, i ^ k) for i in range(lax.axis_size(axis))])

    x = x + other("gy", 1)
    for axis, unit in (("gy", 2), ("gx", 1), ("gx", 4)):
        x = (x + other(axis, unit)) + (other(axis, 2 * unit) + other(axis, 3 * unit))
    return x


def make_transform(gram, proj):
    eye = jnp.eye(MEMBERS, dtype=F32)
    lower = jnp.linalg.cholesky(gram)
    inverse = lax.linalg.triangular_solve(lower, eye, left_side=True, lower=True)
    inner = jnp.dot(inverse, proj, precision=lax.Precision.HIGHEST, preferred_element_type=F32)
    weights = jnp.dot(inverse.T, inner, precision=lax.Precision.HIGHEST, preferred_element_type=F32)
    return (weights[None, :] + jnp.sqrt(F32(MEMBERS - 1)) * inverse).astype(BF16)


def on_device(ensemble, layer_depth, obs_dest, obs_cell, obs_value, obs_sigma):
    et = to_lanes(ensemble)
    from_left = shift(et[:, :, :, COLS - HALO:], "gy", 1)
    from_right = shift(et[:, :, :, :HALO], "gy", -1)
    top = shift(et[:, :, ROWS - HALO:], "gx", 1)
    bottom = shift(et[:, :, :HALO], "gx", -1)
    sides = jnp.concatenate([from_left, from_right], axis=3)
    corner_t = shift(sides[:, :, ROWS - HALO:], "gx", 1)
    corner_b = shift(sides[:, :, :HALO], "gx", -1)

    row0 = lax.axis_index("gx") * ROWS - HALO + jnp.arange(WIDE_ROWS, dtype=jnp.int32)
    col0 = lax.axis_index("gy") * COLS - HALO + jnp.arange(COLS + 2 * HALO, dtype=jnp.int32)
    row_in = (row0 >= 0) & (row0 < lax.axis_size("gx") * ROWS)
    col_in = (col0 >= 0) & (col0 < lax.axis_size("gy") * COLS)
    d = layer_depth
    d = jnp.concatenate(
        [shift(d[:, :, COLS - HALO:], "gy", 1), d, shift(d[:, :, :HALO], "gy", -1)], axis=2
    )
    d = jnp.concatenate(
        [shift(d[:, ROWS - HALO:], "gx", 1), d, shift(d[:, :HALO], "gx", -1)], axis=1
    )
    d = jnp.where(row_in[:, None] & col_in[None, :], HALF * d, 0.0)
    depth = jnp.broadcast_to(d[..., None], d.shape + (MEMBERS,))
    col_scale = jnp.broadcast_to(
        jnp.where(col_in, F32(HALF), F32(0.0))[:, None], (COLS + 2 * HALO, MEMBERS)
    )
    row_scale = row_in.astype(F32)[None, :]

    weight, pull = observed_cells(obs_dest[0, 0], obs_cell[0, 0], obs_value[0, 0], obs_sigma[0, 0])
    weight = jnp.broadcast_to(weight[..., None], (ROWS, COLS, MEMBERS))
    pull = jnp.broadcast_to(pull[..., None], (ROWS, COLS, MEMBERS))

    states = [
        forecast(j, et, sides, top, bottom, corner_t, corner_b, depth, col_scale, row_scale)
        for j in range(CHUNKS)
    ]
    total = sum_everywhere(gram_of(states, weight, pull))
    gram = total[:MEMBERS] + (MEMBERS - 1) * jnp.eye(MEMBERS, dtype=F32)
    return analyse(states, make_transform(gram, total[MEMBERS]))


def solution(mesh):
    in_specs = (
        P(None, None, None, "gx", "gy"),
        P(None, "gx", "gy"),
        P("gx", "gy", None),
        P("gx", "gy", None, None),
        P("gx", "gy", None, None),
        P("gx", "gy", None, None),
    )
    out_specs = P(None, None, None, "gx", "gy")
    return jax.shard_map(
        on_device, mesh=mesh, in_specs=in_specs, out_specs=out_specs, check_vma=False
    )
```

```python
import jax
import jax.numpy as jnp
from jax import lax
from jax.experimental import pallas as pl
from jax.experimental.pallas import tpu as pltpu
from jax.sharding import PartitionSpec as P

MEMBERS = 128
ROWS = 32
COLS = 128
HALO = 8
STEPS = 4
WIDE_ROWS = ROWS + 2 * HALO
WIDE_COLS = COLS + 2 * HALO
SEGMENTS = 16
POSITIONS = WIDE_COLS // SEGMENTS
LINE = 40
LAYERS = 2
HALF = 0.15
TURN = 0.12
COUPLING = 0.5
VMEM = 60 * 1024 * 1024

F32 = jnp.float32
BF16 = jnp.bfloat16


def params():
    return pltpu.CompilerParams(vmem_limit_bytes=VMEM)


def shift(x, axis, by):
    n = lax.axis_size(axis)
    return lax.ppermute(x, axis, [(i, (i + by) % n) for i in range(n)])


def to_lanes(block):
    layers, parts, members, rows, cols = block.shape
    pitch = rows + 1

    def kernel(e_ref, o_ref, planes):
        def spread(m, carry):
            for k in range(4):
                planes[pl.ds((4 * m + k) * pitch, rows), :] = e_ref[0, 0, 4 * m + k].astype(F32)
            return carry

        lax.fori_loop(0, members // 4, spread, 0, unroll=2)

        def turn(x, carry):
            o_ref[0, 0, x] = planes[pl.ds(x, members, stride=pitch), :].astype(BF16).T
            return carry

        lax.fori_loop(0, rows, turn, 0, unroll=4)

    return pl.pallas_call(
        kernel,
        grid=(layers, parts),
        in_specs=[pl.BlockSpec((1, 1, members, rows, cols), lambda i, j: (i, j, 0, 0, 0))],
        out_specs=pl.BlockSpec((1, 1, rows, cols, members), lambda i, j: (i, j, 0, 0, 0)),
        out_shape=jax.ShapeDtypeStruct((layers, parts, rows, cols, members), BF16),
        scratch_shapes=[pltpu.VMEM((members * pitch, cols), F32)],
        compiler_params=params(),
        name="to_lanes_%d" % rows,
    )(block)


def forecast_kernel(
    et, sides, top, bottom, corner_t, corner_b, depth, row_in, masks,
    out, raw, raw_side, st, fx, fy, pr, line, sems,
):
    low, high = pl.ds(0, HALO), pl.ds(HALO + ROWS, HALO)
    copies = []
    for l in range(LAYERS):
        for c in range(3):
            parts = [
                (et.at[l, c], raw.at[l, c, pl.ds(HALO, ROWS)]),
                (top.at[l, c], raw.at[l, c, low]),
                (bottom.at[l, c], raw.at[l, c, high]),
                (sides.at[l, c], raw_side.at[l, c, pl.ds(HALO, ROWS)]),
                (corner_t.at[l, c], raw_side.at[l, c, low]),
                (corner_b.at[l, c], raw_side.at[l, c, high]),
            ]
            copies.append(
                [
                    pltpu.make_async_copy(a, b, sems.at[(3 * l + c) * 6 + k])
                    for k, (a, b) in enumerate(parts)
                ]
            )
    for group in copies:
        for c in group:
            c.start()

    def rolled(x, by):
        return pltpu.roll(x.astype(F32), by % SEGMENTS, 0).astype(BF16)

    def put_flux(l, r, flux):
        fy[l, r, 1:POSITIONS + 1] = flux
        fy[l, r, 0] = rolled(flux[POSITIONS - 1], 1)
        fy[l, r, POSITIONS + 1] = rolled(flux[0], -1)

    def put_pressure(l, r, value):
        pr[l, r, 1:POSITIONS + 1] = value
        pr[l, r, 0] = rolled(value[POSITIONS - 1], 1)
        pr[l, r, POSITIONS + 1] = rolled(value[0], -1)

    for l in range(LAYERS):
        for c in range(3):
            for d in copies[3 * l + c]:
                d.wait()

            def unpack(r, carry):
                scale = HALF if c == 2 else 1.0
                side = raw_side[l, c, r].astype(F32) * scale
                base = lax.rem(r, 4) * (4 * LINE)
                line[pl.ds(base, 8), :] = side[0:8]
                line[pl.ds(base + 8, COLS), :] = raw[l, c, r].astype(F32) * scale
                line[pl.ds(base + 8 + COLS, 8), :] = side[8:16]
                value = jnp.stack(
                    [
                        line[pl.ds(base + p, SEGMENTS, stride=POSITIONS), :].astype(BF16)
                        for p in range(POSITIONS)
                    ],
                    axis=0,
                )
                st[l, c, r] = value
                if c == 0:
                    fx[l, r] = depth[l, r] * value
                elif c == 1:
                    put_flux(l, r, depth[l, r] * value)
                return carry

            lax.fori_loop(0, WIDE_ROWS, unpack, 0, unroll=2)

    for step in range(1, STEPS + 1):

        def thickness(r, carry):
            new = []
            for l in range(LAYERS):
                div = (fx[l, r + 1] - fx[l, r - 1]) + (
                    fy[l, r, 2:POSITIONS + 2] - fy[l, r, 0:POSITIONS]
                )
                h = st[l, 2, r] - div
                st[l, 2, r] = h
                new.append(h)
            mask = masks[row_in[0, r]]
            put_pressure(0, r, (new[0] + new[1]) * mask)
            put_pressure(1, r, (BF16(COUPLING) * new[0] + new[1]) * mask)
            return carry

        lax.fori_loop(2 * step - 1, WIDE_ROWS - (2 * step - 1), thickness, 0)

        def velocity(r, carry):
            for l in range(LAYERS):
                u, v = st[l, 0, r], st[l, 1, r]
                u_new = (u + BF16(TURN) * v) - (
                    pr[l, r + 1, 1:POSITIONS + 1] - pr[l, r - 1, 1:POSITIONS + 1]
                )
                v_new = (v - BF16(TURN) * u) - (
                    pr[l, r, 2:POSITIONS + 2] - pr[l, r, 0:POSITIONS]
                )
                st[l, 0, r] = u_new
                st[l, 1, r] = v_new
                if step < STEPS:
                    d = depth[l, r]
                    fx[l, r] = d * u_new
                    put_flux(l, r, d * v_new)
            return carry

        lax.fori_loop(2 * step, WIDE_ROWS - 2 * step, velocity, 0)

    for l in range(LAYERS):
        for c in range(3):

            def pack(r, carry):
                base = lax.rem(r, 4) * (4 * LINE)
                for p in range(POSITIONS):
                    line[pl.ds(base + p, SEGMENTS, stride=POSITIONS), :] = st[
                        l, c, r + HALO, p
                    ].astype(F32)
                value = line[pl.ds(base + 8, COLS), :]
                if c == 2:
                    value = value * (1.0 / HALF)
                out[l, c, r] = value.astype(BF16)
                return carry

            lax.fori_loop(0, ROWS, pack, 0, unroll=2)


def forecast(et, sides, top, bottom, corner_t, corner_b, depth, row_in, masks):
    plane = (LAYERS, WIDE_ROWS, POSITIONS, SEGMENTS, MEMBERS)
    padded = (LAYERS, WIDE_ROWS, POSITIONS + 2, SEGMENTS, MEMBERS)
    anywhere = pl.BlockSpec(memory_space=pl.ANY)
    vmem = pl.BlockSpec(memory_space=pltpu.VMEM)
    return pl.pallas_call(
        forecast_kernel,
        in_specs=[anywhere] * 6 + [vmem, pl.BlockSpec(memory_space=pltpu.SMEM), vmem],
        out_specs=vmem,
        out_shape=jax.ShapeDtypeStruct((LAYERS, 3, ROWS, COLS, MEMBERS), BF16),
        scratch_shapes=[
            pltpu.VMEM((LAYERS, 3, WIDE_ROWS, COLS, MEMBERS), BF16),
            pltpu.VMEM((LAYERS, 3, WIDE_ROWS, 16, MEMBERS), BF16),
            pltpu.VMEM((LAYERS, 3) + plane[1:], BF16),
            pltpu.VMEM(plane, BF16),
            pltpu.VMEM(padded, BF16),
            pltpu.VMEM(padded, BF16),
            pltpu.VMEM((16 * LINE, MEMBERS), F32),
            pltpu.SemaphoreType.DMA((36,)),
        ],
        compiler_params=params(),
        name="forecast",
    )(et, sides, top, bottom, corner_t, corner_b, depth, row_in, masks)


def gram_kernel(heights, weight, pull, out, high, low):
    def body(x, acc):
        ssh = heights[0, 0, x].astype(F32) + heights[1, 0, x].astype(F32)
        mean = jnp.sum(ssh, axis=1, keepdims=True) * (1.0 / MEMBERS)
        z = ssh - mean
        w = weight[x]
        y = z * jnp.sqrt(w)
        y_high = y.astype(BF16)
        at = pl.ds(pl.multiple_of(x * COLS, COLS), COLS)
        high[at, :] = y_high
        low[at, :] = (y - y_high.astype(F32)).astype(BF16)
        pulled = z * (pull[x] - mean * w)
        return acc + jnp.sum(pulled.reshape(COLS // 8, 8, MEMBERS), axis=0)

    acc = lax.fori_loop(0, ROWS, body, jnp.zeros((8, MEMBERS), F32))
    contract = (((0,), (0,)), ((), ()))
    main = lax.dot_general(high[...], high[...], contract, preferred_element_type=F32)
    cross = lax.dot_general(high[...], low[...], contract, preferred_element_type=F32)
    out[0:MEMBERS, :] = main + (cross + cross.T)
    out[MEMBERS:MEMBERS + 8, :] = jnp.broadcast_to(
        jnp.sum(acc, axis=0, keepdims=True), (8, MEMBERS)
    )


def gram_of(state, weight, pull):
    cells = pl.BlockSpec((ROWS, COLS, MEMBERS), lambda i: (0, 0, 0))
    return pl.pallas_call(
        gram_kernel,
        grid=(1,),
        in_specs=[
            pl.BlockSpec((LAYERS, 1, ROWS, COLS, MEMBERS), lambda i: (0, 2, 0, 0, 0)),
            cells,
            cells,
        ],
        out_specs=pl.BlockSpec((MEMBERS + 8, MEMBERS), lambda i: (0, 0)),
        out_shape=jax.ShapeDtypeStruct((MEMBERS + 8, MEMBERS), F32),
        scratch_shapes=[
            pltpu.VMEM((ROWS * COLS, MEMBERS), BF16),
            pltpu.VMEM((ROWS * COLS, MEMBERS), BF16),
        ],
        compiler_params=params(),
        name="gram",
    )(state, weight, pull)


def analysis_kernel(state, mix, out, planes):
    pitch = ROWS + 1
    over_last = (((1,), (1,)), ((), ()))
    both = mix[...]

    def body(x, carry):
        s = state[0, 0, pl.ds(2 * x, 2)].reshape(2 * COLS, MEMBERS)
        mixed = lax.dot_general(
            both, jnp.concatenate([s, s], axis=1), over_last, preferred_element_type=F32
        )
        planes[pl.ds(2 * x, MEMBERS, stride=pitch), :] = mixed[:, :COLS]
        planes[pl.ds(2 * x + 1, MEMBERS, stride=pitch), :] = mixed[:, COLS:]
        return carry

    lax.fori_loop(0, ROWS // 2, body, 0, unroll=2)

    def gather(m, carry):
        for k in range(4):
            out[0, 0, 4 * m + k] = planes[pl.ds((4 * m + k) * pitch, ROWS), :].astype(BF16)
        return carry

    lax.fori_loop(0, MEMBERS // 4, gather, 0, unroll=2)


def analyse(state, mix):
    return pl.pallas_call(
        analysis_kernel,
        grid=(LAYERS, 3),
        in_specs=[
            pl.BlockSpec((1, 1, ROWS, COLS, MEMBERS), lambda i, j: (i, j, 0, 0, 0)),
            pl.BlockSpec((MEMBERS, 2 * MEMBERS), lambda i, j: (0, 0)),
        ],
        out_specs=pl.BlockSpec((1, 1, MEMBERS, ROWS, COLS), lambda i, j: (i, j, 0, 0, 0)),
        out_shape=jax.ShapeDtypeStruct((LAYERS, 3, MEMBERS, ROWS, COLS), BF16),
        scratch_shapes=[pltpu.VMEM((MEMBERS * (ROWS + 1), COLS), F32)],
        compiler_params=params(),
        name="analysis",
    )(state, mix)


def split3(x):
    a = lax.reduce_precision(x, 8, 7)
    b = lax.reduce_precision(x - a, 8, 7)
    c = lax.reduce_precision(x - a - b, 8, 7)
    return [p.astype(BF16) for p in (a, b, c)]


def observed_cells(dest, cell, value, sigma):
    tiles = lax.axis_size("gy")
    inverse = 1.0 / sigma
    weight = inverse * inverse
    pieces = jnp.stack(split3(weight) + split3(value * weight), 0).reshape(6, -1)
    row = (dest[:, None] * ROWS + cell // COLS).reshape(-1)
    col = (cell % COLS).reshape(-1)
    row_hot = (row[None, :] == jnp.arange(tiles * ROWS, dtype=jnp.int32)[:, None]).astype(BF16)
    col_hot = col[:, None] == jnp.arange(COLS, dtype=jnp.int32)[None, :]
    spread = jnp.where(col_hot[None], pieces[:, :, None], jnp.zeros((), BF16))
    field = jnp.einsum("rk,pkc->prc", row_hot, spread, preferred_element_type=F32)
    field = jnp.stack([field[2] + field[1] + field[0], field[5] + field[4] + field[3]], 0)
    field = field.reshape(2, tiles, ROWS, COLS).transpose(1, 0, 2, 3)
    me = lax.axis_index("gy")
    bit = tiles // 2
    while bit:
        pair = field.reshape((2, bit) + field.shape[1:])
        mine = (me // bit) % 2
        keep = lax.dynamic_index_in_dim(pair, mine, 0, keepdims=False)
        send = lax.dynamic_index_in_dim(pair, 1 - mine, 0, keepdims=False)
        field = keep + lax.ppermute(send, "gy", [(i, i ^ bit) for i in range(tiles)])
        bit //= 2
    return field[0, 0], field[0, 1]


def sum_everywhere(x):
    def other(axis, k):
        return lax.ppermute(x, axis, [(i, i ^ k) for i in range(lax.axis_size(axis))])

    x = x + other("gy", 1)
    for axis, unit in (("gy", 2), ("gx", 1), ("gx", 4)):
        x = (x + other(axis, unit)) + (other(axis, 2 * unit) + other(axis, 3 * unit))
    return x


def make_transform(gram, proj):
    eye = jnp.eye(MEMBERS, dtype=F32)
    lower = jnp.linalg.cholesky(gram)
    inverse = lax.linalg.triangular_solve(lower, eye, left_side=True, lower=True)
    inner = jnp.dot(inverse, proj, precision=lax.Precision.HIGHEST, preferred_element_type=F32)
    weights = jnp.dot(inverse.T, inner, precision=lax.Precision.HIGHEST, preferred_element_type=F32)
    transform_t = weights[None, :] + jnp.sqrt(F32(MEMBERS - 1)) * inverse
    spare = (1.0 - jnp.sum(transform_t, axis=1, keepdims=True)) * (1.0 / MEMBERS)
    mix = transform_t + spare
    high = lax.reduce_precision(mix, 8, 7)
    return jnp.concatenate([high.astype(BF16), (mix - high).astype(BF16)], axis=1)


def on_device(ensemble, layer_depth, obs_dest, obs_cell, obs_value, obs_sigma):
    top = to_lanes(shift(ensemble[:, :, :, ROWS - HALO:], "gx", 1))
    bottom = to_lanes(shift(ensemble[:, :, :, :HALO], "gx", -1))
    et = to_lanes(ensemble)
    from_left = shift(et[:, :, :, COLS - HALO:], "gy", 1)
    from_right = shift(et[:, :, :, :HALO], "gy", -1)
    sides = jnp.concatenate([from_left, from_right], axis=3)
    corner_t = shift(sides[:, :, ROWS - HALO:], "gx", 1)
    corner_b = shift(sides[:, :, :HALO], "gx", -1)

    row0 = lax.axis_index("gx") * ROWS - HALO + jnp.arange(WIDE_ROWS, dtype=jnp.int32)
    col0 = lax.axis_index("gy") * COLS - HALO + jnp.arange(COLS + 2 * HALO, dtype=jnp.int32)
    row_in = (row0 >= 0) & (row0 < lax.axis_size("gx") * ROWS)
    col_in = (col0 >= 0) & (col0 < lax.axis_size("gy") * COLS)
    d = layer_depth
    d = jnp.concatenate(
        [shift(d[:, :, COLS - HALO:], "gy", 1), d, shift(d[:, :, :HALO], "gy", -1)], axis=2
    )
    d = jnp.concatenate(
        [shift(d[:, ROWS - HALO:], "gx", 1), d, shift(d[:, :HALO], "gx", -1)], axis=1
    )
    d = jnp.where(row_in[:, None] & col_in[None, :], (HALF * HALF) * d, 0.0).astype(BF16)
    d = d.reshape(LAYERS, WIDE_ROWS, SEGMENTS, POSITIONS).transpose(0, 1, 3, 2)
    depth = jnp.broadcast_to(d[..., None], d.shape + (MEMBERS,))
    mask = col_in.reshape(SEGMENTS, POSITIONS).T.astype(BF16)
    mask = jnp.stack([jnp.zeros_like(mask), mask], axis=0)
    masks = jnp.broadcast_to(mask[..., None], mask.shape + (MEMBERS,))
    row_in = row_in.astype(jnp.int32)[None, :]

    weight, pull = observed_cells(obs_dest[0, 0], obs_cell[0, 0], obs_value[0, 0], obs_sigma[0, 0])
    weight = jnp.broadcast_to(weight[..., None], (ROWS, COLS, MEMBERS))
    pull = jnp.broadcast_to(pull[..., None], (ROWS, COLS, MEMBERS))

    state = forecast(et, sides, top, bottom, corner_t, corner_b, depth, row_in, masks)
    total = sum_everywhere(gram_of(state, weight, pull))
    gram = total[:MEMBERS] + (MEMBERS - 1) * jnp.eye(MEMBERS, dtype=F32)
    return analyse(state, make_transform(gram, total[MEMBERS]))


def solution(mesh):
    in_specs = (
        P(None, None, None, "gx", "gy"),
        P(None, "gx", "gy"),
        P("gx", "gy", None),
        P("gx", "gy", None, None),
        P("gx", "gy", None, None),
        P("gx", "gy", None, None),
    )
    out_specs = P(None, None, None, "gx", "gy")
    return jax.shard_map(
        on_device, mesh=mesh, in_specs=in_specs, out_specs=out_specs, check_vma=False
    )
```

```python
import jax
import jax.numpy as jnp
from jax import lax
from jax.experimental import pallas as pl
from jax.experimental.pallas import tpu as pltpu
from jax.sharding import PartitionSpec as P

MEMBERS = 128
ROWS = 32
COLS = 128
HALO = 8
STEPS = 4
WIDE_ROWS = ROWS + 2 * HALO
WIDE_COLS = COLS + 2 * HALO
SEGMENTS = 16
POSITIONS = WIDE_COLS // SEGMENTS
LINE = 40
PANEL = 8
LAYERS = 2
HALF = 0.15
TURN = 0.12
COUPLING = 0.5
VMEM = 60 * 1024 * 1024

F32 = jnp.float32
BF16 = jnp.bfloat16


COST = pl.CostEstimate(flops=1, bytes_accessed=1, transcendentals=0)


def params():
    return pltpu.CompilerParams(vmem_limit_bytes=VMEM)


def shift(x, axis, by):
    n = lax.axis_size(axis)
    return lax.ppermute(x, axis, [(i, (i + by) % n) for i in range(n)])


def turn_rows(e_ref, planes, rows, put):
    pitch = ROWS + 1
    tiles = sorted({x // 8 * 8 for x in rows})

    def spread(m, carry):
        for k in range(4):
            plane = e_ref[0, 0, 4 * m + k].astype(F32)
            for lo in tiles:
                planes[pl.ds((4 * m + k) * pitch + lo, 8), :] = plane[lo:lo + 8]
        return carry

    lax.fori_loop(0, MEMBERS // 4, spread, 0, unroll=2)
    for x in rows:
        put(x, planes[pl.ds(x, MEMBERS, stride=pitch), :].astype(BF16).T)


E_BLOCK = pl.BlockSpec((1, 1, MEMBERS, ROWS, COLS), lambda i, j: (i, j, 0, 0, 0))
FAR = 3 * HALO - 2


def edge_rows(ensemble):
    def kernel(e_ref, north, south, planes):
        part = pl.program_id(1)
        base = pl.program_id(0) * FAR + part * (HALO - 1) + (part > 0)

        def put(x, value):
            if x < HALO - 1:
                north[base + x] = value
            elif x > ROWS - HALO:
                south[base + (x - (ROWS - HALO)) - (part > 0)] = value
            else:

                @pl.when(part == 0)
                def _():
                    if x < HALO:
                        north[base + x] = value
                    else:
                        south[base] = value

        rows = list(range(HALO)) + list(range(ROWS - HALO, ROWS))
        turn_rows(e_ref, planes, rows, put)

    whole = pl.BlockSpec((LAYERS * FAR, COLS, MEMBERS), lambda i, j: (0, 0, 0))
    shape = jax.ShapeDtypeStruct((LAYERS * FAR, COLS, MEMBERS), BF16)
    return pl.pallas_call(
        kernel,
        grid=(LAYERS, 3),
        in_specs=[E_BLOCK],
        out_specs=[whole, whole],
        out_shape=[shape, shape],
        scratch_shapes=[pltpu.VMEM((MEMBERS * (ROWS + 1), COLS), F32)],
        compiler_params=params(),
        cost_estimate=COST,
        name="edge_rows",
    )(ensemble)


def all_rows(ensemble, after):
    def kernel(e_ref, after_ref, own, left, right, planes):
        held = {}

        def put(x, value):
            own[0, 0, x] = value
            if x % 2:
                other = held.pop(x - 1)
                left[0, 0, x // 2] = jnp.concatenate([other[:HALO], value[:HALO]], axis=0)
                right[0, 0, x // 2] = jnp.concatenate(
                    [other[COLS - HALO:], value[COLS - HALO:]], axis=0
                )
            else:
                held[x] = value

        turn_rows(e_ref, planes, list(range(ROWS)), put)

    def whole(block):
        return jax.ShapeDtypeStruct((LAYERS, 3) + block[2:], BF16)

    def spec(block):
        return pl.BlockSpec(block, lambda i, j: (i, j, 0, 0, 0))

    tile = (1, 1, ROWS, COLS, MEMBERS)
    side = (1, 1, ROWS // 2, 16, MEMBERS)
    return pl.pallas_call(
        kernel,
        grid=(LAYERS, 3),
        in_specs=[E_BLOCK, pl.BlockSpec(memory_space=pl.ANY)],
        out_specs=[spec(tile), spec(side), spec(side)],
        out_shape=[whole(tile), whole(side), whole(side)],
        scratch_shapes=[pltpu.VMEM((MEMBERS * (ROWS + 1), COLS), F32)],
        compiler_params=params(),
        cost_estimate=COST,
        name="all_rows",
    )(ensemble, after)


def forecast_kernel(
    own, top, bottom, left, right, corner_t, corner_b, depth_in, row_in, masks,
    out, raw, raw_side, depth, st, fx, fy, pr, line, sems,
):
    depth_copy = pltpu.make_async_copy(depth_in, depth, sems.at[54])
    depth_copy.start()
    order = [(l, c) for l in range(LAYERS) for c in range(3)]
    copies = {}
    for l, c in order:
        count = HALO - (c > 0)
        at = pl.ds(l * FAR + c * (HALO - 1) + (c > 0), count)
        rows = [
            (own.at[l, c], raw.at[l, c, pl.ds(HALO, ROWS)]),
            (top.at[at], raw.at[l, c, pl.ds(HALO - count, count)]),
            (bottom.at[at], raw.at[l, c, pl.ds(HALO + ROWS, count)]),
        ]
        for k, piece in enumerate((left, right)):
            rows.append((piece.at[l, c], raw_side.at[k, l, c, pl.ds(4, 16)]))
            rows.append((corner_t.at[k, l, c], raw_side.at[k, l, c, pl.ds(0, 4)]))
            rows.append((corner_b.at[k, l, c], raw_side.at[k, l, c, pl.ds(20, 4)]))
        copies[l, c] = [
            pltpu.make_async_copy(x, y, sems.at[(3 * l + c) * 9 + k])
            for k, (x, y) in enumerate(rows)
        ]
    for key in order:
        for c in copies[key]:
            c.start()
    depth_copy.wait()

    def rolled(x, by):
        return pltpu.roll(x.astype(F32), by % SEGMENTS, 0).astype(BF16)

    def put_flux(l, r, flux):
        fy[l, r, 1:POSITIONS + 1] = flux
        fy[l, r, 0] = rolled(flux[POSITIONS - 1], 1)
        fy[l, r, POSITIONS + 1] = rolled(flux[0], -1)

    def put_pressure(l, r, value):
        pr[l, r, 1:POSITIONS + 1] = value
        pr[l, r, 0] = rolled(value[POSITIONS - 1], 1)
        pr[l, r, POSITIONS + 1] = rolled(value[0], -1)

    for l, c in order:
        for d in copies[l, c]:
            d.wait()

        def unpack(pair, carry):
            scale = HALF if c == 2 else 1.0
            sides = [raw_side[k, l, c, pair].astype(F32) * scale for k in range(2)]
            for odd in range(2):
                r = 2 * pair + odd
                base = lax.rem(pair, 2) * (8 * LINE) + odd * (4 * LINE)
                half = slice(8 * odd, 8 * odd + 8)
                line[pl.ds(base, 8), :] = sides[0][half]
                line[pl.ds(base + 8, COLS), :] = raw[l, c, r].astype(F32) * scale
                line[pl.ds(base + 8 + COLS, 8), :] = sides[1][half]
                value = jnp.stack(
                    [
                        line[pl.ds(base + p, SEGMENTS, stride=POSITIONS), :].astype(BF16)
                        for p in range(POSITIONS)
                    ],
                    axis=0,
                )
                st[l, c, r] = value
                if c == 0:
                    fx[l, r] = depth[l, r] * value
                elif c == 1:
                    put_flux(l, r, depth[l, r] * value)
            return carry

        lax.fori_loop(0, WIDE_ROWS // 2, unpack, 0)

    mid = slice(1, POSITIONS + 1)

    def sweep(body, rows_from, rows_to, first):
        for start in (rows_from, rows_from + 1):
            lax.fori_loop(
                0,
                (rows_to - rows_from) // 2,
                lambda i, above, start=start: body(start + 2 * i, above),
                first(start),
                unroll=2,
            )

    for step in range(1, STEPS + 1):

        def thickness(r, above):
            new, below = [], []
            for l in range(LAYERS):
                nxt = fx[l, r + 1]
                g = fy[l, r]
                h = st[l, 2, r] - ((nxt - above[l]) + (g[2:] - g[:POSITIONS]))
                st[l, 2, r] = h
                new.append(h)
                below.append(nxt)
            mask = masks[row_in[0, r]]
            put_pressure(0, r, (new[0] + new[1]) * mask)
            put_pressure(1, r, (BF16(COUPLING) * new[0] + new[1]) * mask)
            return tuple(below)

        sweep(
            thickness, 2 * step - 1, WIDE_ROWS - (2 * step - 1),
            lambda r: tuple(fx[l, r - 1] for l in range(LAYERS)),
        )

        def velocity(r, above):
            below = []
            for l in range(LAYERS):
                u, v = st[l, 0, r], st[l, 1, r]
                nxt = pr[l, r + 1, mid]
                g = pr[l, r]
                u_new = (u + BF16(TURN) * v) - (nxt - above[l])
                v_new = (v - BF16(TURN) * u) - (g[2:] - g[:POSITIONS])
                st[l, 0, r] = u_new
                st[l, 1, r] = v_new
                if step < STEPS:
                    d = depth[l, r]
                    fx[l, r] = d * u_new
                    put_flux(l, r, d * v_new)
                below.append(nxt)
            return tuple(below)

        sweep(
            velocity, 2 * step, WIDE_ROWS - 2 * step,
            lambda r: tuple(pr[l, r - 1, mid] for l in range(LAYERS)),
        )

    done = []
    for l in range(LAYERS):
        for c in range(3):

            def pack(r, carry):
                base = lax.rem(r, 4) * (4 * LINE)
                for p in range(POSITIONS):
                    line[pl.ds(base + p, SEGMENTS, stride=POSITIONS), :] = st[
                        l, c, r + HALO, p
                    ].astype(F32)
                value = line[pl.ds(base + 8, COLS), :]
                if c == 2:
                    value = value * (1.0 / HALF)
                raw[l, c, r] = value.astype(BF16)
                return carry

            lax.fori_loop(0, ROWS, pack, 0, unroll=2)
            done.append(
                pltpu.make_async_copy(
                    raw.at[l, c, pl.ds(0, ROWS)], out.at[l, c], sems.at[55 + 3 * l + c]
                )
            )
            done[-1].start()
    for d in done:
        d.wait()


def forecast(*operands):
    plane = (LAYERS, WIDE_ROWS, POSITIONS, SEGMENTS, MEMBERS)
    padded = (LAYERS, WIDE_ROWS, POSITIONS + 2, SEGMENTS, MEMBERS)
    anywhere = pl.BlockSpec(memory_space=pl.ANY)
    vmem = pl.BlockSpec(memory_space=pltpu.VMEM)
    return pl.pallas_call(
        forecast_kernel,
        in_specs=[anywhere] * 8 + [pl.BlockSpec(memory_space=pltpu.SMEM), vmem],
        out_specs=anywhere,
        out_shape=jax.ShapeDtypeStruct((LAYERS, 3, ROWS, COLS, MEMBERS), BF16),
        scratch_shapes=[
            pltpu.VMEM((LAYERS, 3, WIDE_ROWS, COLS, MEMBERS), BF16),
            pltpu.VMEM((2, LAYERS, 3, WIDE_ROWS // 2, 16, MEMBERS), BF16),
            pltpu.VMEM(plane, BF16),
            pltpu.VMEM((LAYERS, 3) + plane[1:], BF16),
            pltpu.VMEM(plane, BF16),
            pltpu.VMEM(padded, BF16),
            pltpu.VMEM(padded, BF16),
            pltpu.VMEM((16 * LINE, MEMBERS), F32),
            pltpu.SemaphoreType.DMA((61,)),
        ],
        compiler_params=params(),
        cost_estimate=COST,
        name="forecast",
    )(*operands)


def gram_kernel(heights, weight, pull, out, left, right, acc):
    n = MEMBERS
    over_last = (((1,), (1,)), ((), ()))
    eye = lax.broadcasted_iota(jnp.int32, (n, n), 0) == lax.broadcasted_iota(jnp.int32, (n, n), 1)
    away = (eye.astype(F32) - 1.0 / n).astype(BF16)
    away = jnp.concatenate([away, away], axis=1)
    share = jnp.full((8, 2 * n), 1.0 / n, BF16)
    acc[...] = jnp.zeros_like(acc)

    def body(x, carry):
        both = jnp.concatenate([heights[0, 0, x], heights[1, 0, x]], axis=1)
        z = lax.dot_general(both, away, over_last, preferred_element_type=F32)
        zt = lax.dot_general(away, both, over_last, preferred_element_type=F32)
        mean = lax.dot_general(share, both, over_last, preferred_element_type=F32)[0:1]
        w = weight[pl.ds(x, 1), :]
        y = zt * w
        at = pl.ds(pl.multiple_of(x * COLS, COLS), COLS)
        y_high = y.astype(BF16)
        z_high = z.astype(BF16)
        left[0, x] = y_high
        left[1, x] = (y - y_high.astype(F32)).astype(BF16)
        right[x, :, 0:n] = z_high
        right[x, :, n:2 * n] = (z - z_high.astype(F32)).astype(BF16)
        acc[...] += zt * (pull[pl.ds(x, 1), :] - mean * w)
        return carry

    lax.fori_loop(0, ROWS, body, 0, unroll=2)

    def multiply(x, total):
        a = jnp.concatenate([left[0, 2 * x], left[0, 2 * x + 1]], axis=1)
        b = jnp.concatenate([left[1, 2 * x], left[1, 2 * x + 1]], axis=1)
        z = right[pl.ds(2 * x, 2)].reshape(2 * COLS, 2 * n)
        main = jnp.dot(a, z, preferred_element_type=F32)
        low = jnp.dot(b, z[:, 0:n], preferred_element_type=F32)
        return total + (main[:, 0:n] + (main[:, n:2 * n] + low))

    out[0:n, :] = lax.fori_loop(0, ROWS // 2, multiply, jnp.zeros((n, n), F32), unroll=2)
    out[n:n + 8, :] = jnp.broadcast_to(jnp.sum(acc[...].T, axis=0, keepdims=True), (8, n))


def gram_of(state, weight, pull):
    cells = pl.BlockSpec((ROWS, COLS), lambda i: (0, 0))
    return pl.pallas_call(
        gram_kernel,
        grid=(1,),
        in_specs=[
            pl.BlockSpec((LAYERS, 1, ROWS, COLS, MEMBERS), lambda i: (0, 2, 0, 0, 0)),
            cells,
            cells,
        ],
        out_specs=pl.BlockSpec((MEMBERS + 8, MEMBERS), lambda i: (0, 0)),
        out_shape=jax.ShapeDtypeStruct((MEMBERS + 8, MEMBERS), F32),
        scratch_shapes=[
            pltpu.VMEM((2, ROWS, MEMBERS, COLS), BF16),
            pltpu.VMEM((ROWS, COLS, 2 * MEMBERS), BF16),
            pltpu.VMEM((MEMBERS, COLS), F32),
        ],
        compiler_params=params(),
        cost_estimate=COST,
        name="gram",
    )(state, weight, pull)


def analysis_kernel(state, mix, out, planes):
    pitch = ROWS + 1
    over_last = (((1,), (1,)), ((), ()))
    both = mix[...]

    def body(x, carry):
        s = state[0, 0, pl.ds(2 * x, 2)].reshape(2 * COLS, MEMBERS)
        mixed = lax.dot_general(
            both, jnp.concatenate([s, s], axis=1), over_last, preferred_element_type=F32
        )
        planes[pl.ds(2 * x, MEMBERS, stride=pitch), :] = mixed[:, :COLS]
        planes[pl.ds(2 * x + 1, MEMBERS, stride=pitch), :] = mixed[:, COLS:]
        return carry

    lax.fori_loop(0, ROWS // 2, body, 0, unroll=2)

    def gather(m, carry):
        for k in range(4):
            out[0, 0, 4 * m + k] = planes[pl.ds((4 * m + k) * pitch, ROWS), :].astype(BF16)
        return carry

    lax.fori_loop(0, MEMBERS // 4, gather, 0, unroll=2)


def analyse(state, mix):
    return pl.pallas_call(
        analysis_kernel,
        grid=(LAYERS, 3),
        in_specs=[
            pl.BlockSpec((1, 1, ROWS, COLS, MEMBERS), lambda i, j: (i, j, 0, 0, 0)),
            pl.BlockSpec((MEMBERS, 2 * MEMBERS), lambda i, j: (0, 0)),
        ],
        out_specs=pl.BlockSpec((1, 1, MEMBERS, ROWS, COLS), lambda i, j: (i, j, 0, 0, 0)),
        out_shape=jax.ShapeDtypeStruct((LAYERS, 3, MEMBERS, ROWS, COLS), BF16),
        scratch_shapes=[pltpu.VMEM((MEMBERS * (ROWS + 1), COLS), F32)],
        compiler_params=params(),
        cost_estimate=COST,
        name="analysis",
    )(state, mix)


def split3(x):
    a = lax.reduce_precision(x, 8, 7)
    b = lax.reduce_precision(x - a, 8, 7)
    c = lax.reduce_precision(x - a - b, 8, 7)
    return [p.astype(BF16) for p in (a, b, c)]


def observed_cells(dest, cell, value, sigma):
    tiles = lax.axis_size("gy")
    inverse = 1.0 / sigma
    weight = inverse * inverse
    pieces = jnp.stack(split3(weight) + split3(value * weight), 0).reshape(6, -1)
    row = ((dest ^ lax.axis_index("gy"))[:, None] * ROWS + cell // COLS).reshape(-1)
    col = (cell % COLS).reshape(-1)
    row_hot = (row[None, :] == jnp.arange(tiles * ROWS, dtype=jnp.int32)[:, None]).astype(BF16)
    col_hot = col[:, None] == jnp.arange(COLS, dtype=jnp.int32)[None, :]
    spread = jnp.where(col_hot[None], pieces[:, :, None], jnp.zeros((), BF16))
    field = jnp.einsum("rk,pkc->prc", row_hot, spread, preferred_element_type=F32)
    field = jnp.stack([field[2] + field[1] + field[0], field[5] + field[4] + field[3]], 0)
    field = field.reshape(2, tiles, ROWS, COLS).transpose(1, 0, 2, 3)
    bit = tiles // 2
    while bit:
        swap = [(i, i ^ bit) for i in range(tiles)]
        field = field[:bit] + lax.ppermute(field[bit:], "gy", swap)
        bit //= 2
    return field[0, 0], field[0, 1]


def sum_everywhere(x):
    def other(axis, k):
        return lax.ppermute(x, axis, [(i, i ^ k) for i in range(lax.axis_size(axis))])

    x = x + other("gy", 1)
    for axis, unit in (("gy", 2), ("gx", 1), ("gx", 4)):
        x = (x + other(axis, unit)) + (other(axis, 2 * unit) + other(axis, 3 * unit))
    return x


def transform_kernel(total, mix, work, inverse):
    n = MEMBERS
    full = lax.Precision.HIGHEST
    rows_i = lax.broadcasted_iota(jnp.int32, (n, n), 0)
    cols_i = lax.broadcasted_iota(jnp.int32, (n, n), 1)
    eye = (rows_i == cols_i).astype(F32)
    work[:, 0:n] = total[0:n, :] + F32(n - 1) * eye
    work[:, n:2 * n] = eye
    sub = lax.broadcasted_iota(jnp.int32, (PANEL, n), 0)
    for first in range(0, n, PANEL):
        rows = slice(first, first + PANEL)
        up, inv = work[rows, 0:n], work[rows, n:2 * n]
        cols = [jnp.broadcast_to(up[:, first + k:first + k + 1], (PANEL, n)) for k in range(PANEL)]
        scale = jnp.zeros((PANEL, n), F32)
        for k in range(PANEL):
            pivot = cols[k][k:k + 1]
            scale = jnp.where(sub == k, pivot, scale)
            if k + 1 < PANEL:
                times = jnp.where(sub > k, cols[k], 0.0) * (1.0 / pivot)
                for q in range(k + 1, PANEL):
                    cols[q] = cols[q] - times * cols[q][k:k + 1]
                up = up - times * up[k:k + 1]
                inv = inv - times * inv[k:k + 1]
        scale = lax.rsqrt(scale)
        up, inv = up * scale, inv * scale
        inverse[rows, :] = inv
        after = first + PANEL
        if after < n:
            update = lax.dot_general(
                up, jnp.concatenate([up, inv], axis=1), (((0,), (0,)), ((), ())),
                precision=full, preferred_element_type=F32,
            )
            work[after:, :] = work[after:, :] - update[after:, :]
    low = inverse[...]
    proj = total[n:n + 8, :]
    inner = lax.dot_general(proj, low, (((1,), (1,)), ((), ())), precision=full, preferred_element_type=F32)
    weights = jnp.dot(inner, low, precision=full, preferred_element_type=F32)
    transform_t = weights[0:1] + F32((n - 1) ** 0.5) * low
    spare = (1.0 - jnp.sum(transform_t, axis=1, keepdims=True)) * (1.0 / n)
    value = transform_t + spare
    high = value.astype(BF16)
    mix[:, 0:n] = high
    mix[:, n:2 * n] = (value - high.astype(F32)).astype(BF16)


def make_mix(total):
    vmem = pl.BlockSpec(memory_space=pltpu.VMEM)
    return pl.pallas_call(
        transform_kernel,
        in_specs=[vmem],
        out_specs=vmem,
        out_shape=jax.ShapeDtypeStruct((MEMBERS, 2 * MEMBERS), BF16),
        scratch_shapes=[
            pltpu.VMEM((MEMBERS, 2 * MEMBERS), F32),
            pltpu.VMEM((MEMBERS, MEMBERS), F32),
        ],
        compiler_params=params(),
        cost_estimate=COST,
        name="transform",
    )(total)


def on_device(ensemble, layer_depth, obs_dest, obs_cell, obs_value, obs_sigma):
    row0 = lax.axis_index("gx") * ROWS - HALO + jnp.arange(WIDE_ROWS, dtype=jnp.int32)
    col0 = lax.axis_index("gy") * COLS - HALO + jnp.arange(COLS + 2 * HALO, dtype=jnp.int32)
    row_in = (row0 >= 0) & (row0 < lax.axis_size("gx") * ROWS)
    col_in = (col0 >= 0) & (col0 < lax.axis_size("gy") * COLS)
    d = layer_depth
    d = jnp.concatenate(
        [shift(d[:, :, COLS - HALO:], "gy", 1), d, shift(d[:, :, :HALO], "gy", -1)], axis=2
    )
    d = jnp.concatenate(
        [shift(d[:, ROWS - HALO:], "gx", 1), d, shift(d[:, :HALO], "gx", -1)], axis=1
    )
    d, north, south = lax.optimization_barrier((d,) + tuple(edge_rows(ensemble)))
    top = shift(south, "gx", 1)
    bottom = shift(north, "gx", -1)
    own, left_out, right_out = all_rows(ensemble, north)
    left = shift(right_out, "gy", 1)
    right = shift(left_out, "gy", -1)
    d = jnp.where(row_in[:, None] & col_in[None, :], (HALF * HALF) * d, 0.0).astype(BF16)
    d = d.reshape(LAYERS, WIDE_ROWS, SEGMENTS, POSITIONS).transpose(0, 1, 3, 2)
    depth = jnp.broadcast_to(d[..., None], d.shape + (MEMBERS,))
    mask = col_in.reshape(SEGMENTS, POSITIONS).T.astype(BF16)
    mask = jnp.stack([jnp.zeros_like(mask), mask], axis=0)
    masks = jnp.broadcast_to(mask[..., None], mask.shape + (MEMBERS,))
    row_in = row_in.astype(jnp.int32)[None, :]
    sides = jnp.stack([left, right], axis=0)
    sides, depth, masks = lax.optimization_barrier((sides, depth, masks))
    corner_t = shift(sides[:, :, :, 12:], "gx", 1)
    corner_b = shift(sides[:, :, :, :4], "gx", -1)

    weight, pull = observed_cells(obs_dest[0, 0], obs_cell[0, 0], obs_value[0, 0], obs_sigma[0, 0])
    state = forecast(
        own, top, bottom, left, right, corner_t, corner_b, depth, row_in, masks
    )
    total = sum_everywhere(gram_of(state, weight, pull))
    return analyse(state, make_mix(total))


def solution(mesh):
    in_specs = (
        P(None, None, None, "gx", "gy"),
        P(None, "gx", "gy"),
        P("gx", "gy", None),
        P("gx", "gy", None, None),
        P("gx", "gy", None, None),
        P("gx", "gy", None, None),
    )
    out_specs = P(None, None, None, "gx", "gy")
    return jax.shard_map(
        on_device, mesh=mesh, in_specs=in_specs, out_specs=out_specs, check_vma=False
    )
```

```python
import jax
import jax.numpy as jnp
from jax import lax
from jax.experimental import pallas as pl
from jax.experimental.pallas import tpu as pltpu
from jax.sharding import PartitionSpec as P

MEMBERS = 128
ROWS = 32
COLS = 128
HALO = 8
STEPS = 4
WIDE_ROWS = ROWS + 2 * HALO
WIDE_COLS = COLS + 2 * HALO
SEGMENTS = 16
POSITIONS = WIDE_COLS // SEGMENTS
LINE = 40
PANEL = 8
LAYERS = 2
HALF = 0.15
TURN = 0.12
COUPLING = 0.5
VMEM = 60 * 1024 * 1024

F32 = jnp.float32
BF16 = jnp.bfloat16


COST = pl.CostEstimate(flops=1, bytes_accessed=1, transcendentals=0)


def params():
    return pltpu.CompilerParams(vmem_limit_bytes=VMEM)


def shift(x, axis, by):
    n = lax.axis_size(axis)
    return lax.ppermute(x, axis, [(i, (i + by) % n) for i in range(n)])


def turn_rows(e_ref, planes, rows, put):
    pitch = ROWS + 1
    tiles = sorted({x // 8 * 8 for x in rows})

    def spread(m, carry):
        for k in range(4):
            plane = e_ref[0, 0, 4 * m + k].astype(F32)
            for lo in tiles:
                planes[pl.ds((4 * m + k) * pitch + lo, 8), :] = plane[lo:lo + 8]
        return carry

    lax.fori_loop(0, MEMBERS // 4, spread, 0, unroll=2)
    for x in rows:
        put(x, planes[pl.ds(x, MEMBERS, stride=pitch), :].astype(BF16).T)


E_BLOCK = pl.BlockSpec((1, 1, MEMBERS, ROWS, COLS), lambda i, j: (i, j, 0, 0, 0))
FAR = 3 * HALO - 2


def all_rows(ensemble):
    def kernel(e_ref, own, left, right, north, south, planes):
        part = pl.program_id(1)
        base = pl.program_id(0) * FAR + part * (HALO - 1) + (part > 0)
        held = {}

        def put(x, value):
            own[0, 0, x] = value
            if x % 2:
                other = held.pop(x - 1)
                left[0, 0, x // 2] = jnp.concatenate([other[:HALO], value[:HALO]], axis=0)
                right[0, 0, x // 2] = jnp.concatenate(
                    [other[COLS - HALO:], value[COLS - HALO:]], axis=0
                )
            else:
                held[x] = value
            if x < HALO - 1:
                north[base + x] = value
            elif x > ROWS - HALO:
                south[base + (x - (ROWS - HALO)) - (part > 0)] = value
            elif x == HALO - 1:

                @pl.when(part == 0)
                def _():
                    north[base + x] = value

            elif x == ROWS - HALO:

                @pl.when(part == 0)
                def _():
                    south[base] = value

        turn_rows(e_ref, planes, list(range(ROWS)), put)

    def whole(block):
        return jax.ShapeDtypeStruct((LAYERS, 3) + block[2:], BF16)

    def spec(block):
        return pl.BlockSpec(block, lambda i, j: (i, j, 0, 0, 0))

    tile = (1, 1, ROWS, COLS, MEMBERS)
    side = (1, 1, ROWS // 2, 16, MEMBERS)
    edge = (LAYERS * FAR, COLS, MEMBERS)
    edge_spec = pl.BlockSpec(edge, lambda i, j: (0, 0, 0))
    edge_shape = jax.ShapeDtypeStruct(edge, BF16)
    return pl.pallas_call(
        kernel,
        grid=(LAYERS, 3),
        in_specs=[E_BLOCK],
        out_specs=[spec(tile), spec(side), spec(side), edge_spec, edge_spec],
        out_shape=[whole(tile), whole(side), whole(side), edge_shape, edge_shape],
        scratch_shapes=[pltpu.VMEM((MEMBERS * (ROWS + 1), COLS), F32)],
        compiler_params=params(),
        cost_estimate=COST,
        name="all_rows",
    )(ensemble)


def forecast_kernel(
    own, top, bottom, left, right, corner_t, corner_b, depth_in, row_in, masks, weight, pull,
    out, total, raw, raw_side, depth, st, fx, fy, pr, line, y_parts, z_parts, acc, sems,
):
    depth_copy = pltpu.make_async_copy(depth_in, depth, sems.at[54])
    depth_copy.start()
    order = [(l, c) for l in range(LAYERS) for c in range(3)]
    copies = {}
    for l, c in order:
        count = HALO - (c > 0)
        at = pl.ds(l * FAR + c * (HALO - 1) + (c > 0), count)
        rows = [
            (own.at[l, c], raw.at[l, c, pl.ds(HALO, ROWS)]),
            (top.at[at], raw.at[l, c, pl.ds(HALO - count, count)]),
            (bottom.at[at], raw.at[l, c, pl.ds(HALO + ROWS, count)]),
        ]
        for k, piece in enumerate((left, right)):
            rows.append((piece.at[l, c], raw_side.at[k, l, c, pl.ds(4, 16)]))
            rows.append((corner_t.at[k, l, c], raw_side.at[k, l, c, pl.ds(0, 4)]))
            rows.append((corner_b.at[k, l, c], raw_side.at[k, l, c, pl.ds(20, 4)]))
        copies[l, c] = [
            pltpu.make_async_copy(x, y, sems.at[(3 * l + c) * 9 + k])
            for k, (x, y) in enumerate(rows)
        ]
    for key in order:
        for c in copies[key]:
            c.start()
    depth_copy.wait()

    def rolled(x, by):
        return pltpu.roll(x.astype(F32), by % SEGMENTS, 0).astype(BF16)

    def put_flux(l, r, flux):
        fy[l, r, 1:POSITIONS + 1] = flux
        fy[l, r, 0] = rolled(flux[POSITIONS - 1], 1)
        fy[l, r, POSITIONS + 1] = rolled(flux[0], -1)

    def put_pressure(l, r, value):
        pr[l, r, 1:POSITIONS + 1] = value
        pr[l, r, 0] = rolled(value[POSITIONS - 1], 1)
        pr[l, r, POSITIONS + 1] = rolled(value[0], -1)

    for l, c in order:
        for d in copies[l, c]:
            d.wait()

        def unpack(pair, carry):
            scale = HALF if c == 2 else 1.0
            sides = [raw_side[k, l, c, pair].astype(F32) * scale for k in range(2)]
            for odd in range(2):
                r = 2 * pair + odd
                base = lax.rem(pair, 2) * (8 * LINE) + odd * (4 * LINE)
                half = slice(8 * odd, 8 * odd + 8)
                line[pl.ds(base, 8), :] = sides[0][half]
                line[pl.ds(base + 8, COLS), :] = raw[l, c, r].astype(F32) * scale
                line[pl.ds(base + 8 + COLS, 8), :] = sides[1][half]
                value = jnp.stack(
                    [
                        line[pl.ds(base + p, SEGMENTS, stride=POSITIONS), :].astype(BF16)
                        for p in range(POSITIONS)
                    ],
                    axis=0,
                )
                st[l, c, r] = value
                if c == 0:
                    fx[l, r] = depth[l, r] * value
                elif c == 1:
                    put_flux(l, r, depth[l, r] * value)
            return carry

        lax.fori_loop(0, WIDE_ROWS // 2, unpack, 0)

    mid = slice(1, POSITIONS + 1)

    def sweep(body, rows_from, rows_to, first):
        for start in (rows_from, rows_from + 1):
            lax.fori_loop(
                0,
                (rows_to - rows_from) // 2,
                lambda i, above, start=start: body(start + 2 * i, above),
                first(start),
                unroll=2,
            )

    for step in range(1, STEPS + 1):

        def thickness(r, above):
            new, below = [], []
            for l in range(LAYERS):
                nxt = fx[l, r + 1]
                g = fy[l, r]
                h = st[l, 2, r] - ((nxt - above[l]) + (g[2:] - g[:POSITIONS]))
                st[l, 2, r] = h
                new.append(h)
                below.append(nxt)
            mask = masks[row_in[0, r]]
            put_pressure(0, r, (new[0] + new[1]) * mask)
            put_pressure(1, r, (BF16(COUPLING) * new[0] + new[1]) * mask)
            return tuple(below)

        sweep(
            thickness, 2 * step - 1, WIDE_ROWS - (2 * step - 1),
            lambda r: tuple(fx[l, r - 1] for l in range(LAYERS)),
        )

        def velocity(r, above):
            below = []
            for l in range(LAYERS):
                u, v = st[l, 0, r], st[l, 1, r]
                nxt = pr[l, r + 1, mid]
                g = pr[l, r]
                u_new = (u + BF16(TURN) * v) - (nxt - above[l])
                v_new = (v - BF16(TURN) * u) - (g[2:] - g[:POSITIONS])
                st[l, 0, r] = u_new
                st[l, 1, r] = v_new
                if step < STEPS:
                    d = depth[l, r]
                    fx[l, r] = d * u_new
                    put_flux(l, r, d * v_new)
                below.append(nxt)
            return tuple(below)

        sweep(
            velocity, 2 * step, WIDE_ROWS - 2 * step,
            lambda r: tuple(pr[l, r - 1, mid] for l in range(LAYERS)),
        )

    done = []
    for c in (2, 0, 1):
        for l in range(LAYERS):

            def pack(r, carry):
                base = lax.rem(r, 4) * (4 * LINE)
                for p in range(POSITIONS):
                    line[pl.ds(base + p, SEGMENTS, stride=POSITIONS), :] = st[
                        l, c, r + HALO, p
                    ].astype(F32)
                value = line[pl.ds(base + 8, COLS), :]
                if c == 2:
                    value = value * (1.0 / HALF)
                raw[l, c, r] = value.astype(BF16)
                return carry

            lax.fori_loop(0, ROWS, pack, 0, unroll=2)
            done.append(
                pltpu.make_async_copy(
                    raw.at[l, c, pl.ds(0, ROWS)], out.at[l, c], sems.at[55 + 3 * l + c]
                )
            )
            done[-1].start()
    add_up(raw, weight, pull, total, y_parts, z_parts, acc)
    for d in done:
        d.wait()


def add_up(state, weight, pull, total, left, right, acc):
    n = MEMBERS
    over_last = (((1,), (1,)), ((), ()))
    eye = lax.broadcasted_iota(jnp.int32, (n, n), 0) == lax.broadcasted_iota(jnp.int32, (n, n), 1)
    away = (eye.astype(F32) - 1.0 / n).astype(BF16)
    away = jnp.concatenate([away, away], axis=1)
    share = jnp.full((8, 2 * n), 1.0 / n, BF16)
    acc[...] = jnp.zeros_like(acc)

    def body(x, carry):
        both = jnp.concatenate([state[0, 2, x], state[1, 2, x]], axis=1)
        z = lax.dot_general(both, away, over_last, preferred_element_type=F32)
        zt = lax.dot_general(away, both, over_last, preferred_element_type=F32)
        mean = lax.dot_general(share, both, over_last, preferred_element_type=F32)[0:1]
        w = weight[pl.ds(x, 1), :]
        y = zt * w
        y_high = y.astype(BF16)
        z_high = z.astype(BF16)
        left[0, x] = y_high
        left[1, x] = (y - y_high.astype(F32)).astype(BF16)
        right[x, :, 0:n] = z_high
        right[x, :, n:2 * n] = (z - z_high.astype(F32)).astype(BF16)
        acc[...] += zt * (pull[pl.ds(x, 1), :] - mean * w)
        return carry

    lax.fori_loop(0, ROWS, body, 0, unroll=4)

    def multiply(x, part):
        a = jnp.concatenate([left[0, 2 * x], left[0, 2 * x + 1]], axis=1)
        b = jnp.concatenate([left[1, 2 * x], left[1, 2 * x + 1]], axis=1)
        z = right[pl.ds(2 * x, 2)].reshape(2 * COLS, 2 * n)
        main = jnp.dot(a, z, preferred_element_type=F32)
        low = jnp.dot(b, z[:, 0:n], preferred_element_type=F32)
        return part + (main[:, 0:n] + (main[:, n:2 * n] + low))

    total[0:n, :] = lax.fori_loop(0, ROWS // 2, multiply, jnp.zeros((n, n), F32), unroll=2)
    total[n:n + 8, :] = jnp.broadcast_to(jnp.sum(acc[...].T, axis=0, keepdims=True), (8, n))


def forecast(*operands):
    plane = (LAYERS, WIDE_ROWS, POSITIONS, SEGMENTS, MEMBERS)
    padded = (LAYERS, WIDE_ROWS, POSITIONS + 2, SEGMENTS, MEMBERS)
    anywhere = pl.BlockSpec(memory_space=pl.ANY)
    vmem = pl.BlockSpec(memory_space=pltpu.VMEM)
    return pl.pallas_call(
        forecast_kernel,
        in_specs=[anywhere] * 8 + [pl.BlockSpec(memory_space=pltpu.SMEM), vmem, vmem, vmem],
        out_specs=[anywhere, vmem],
        out_shape=[
            jax.ShapeDtypeStruct((LAYERS, 3, ROWS, COLS, MEMBERS), BF16),
            jax.ShapeDtypeStruct((MEMBERS + 8, MEMBERS), F32),
        ],
        scratch_shapes=[
            pltpu.VMEM((LAYERS, 3, WIDE_ROWS, COLS, MEMBERS), BF16),
            pltpu.VMEM((2, LAYERS, 3, WIDE_ROWS // 2, 16, MEMBERS), BF16),
            pltpu.VMEM(plane, BF16),
            pltpu.VMEM((LAYERS, 3) + plane[1:], BF16),
            pltpu.VMEM(plane, BF16),
            pltpu.VMEM(padded, BF16),
            pltpu.VMEM(padded, BF16),
            pltpu.VMEM((16 * LINE, MEMBERS), F32),
            pltpu.VMEM((2, ROWS, MEMBERS, COLS), BF16),
            pltpu.VMEM((ROWS, COLS, 2 * MEMBERS), BF16),
            pltpu.VMEM((MEMBERS, COLS), F32),
            pltpu.SemaphoreType.DMA((61,)),
        ],
        compiler_params=params(),
        cost_estimate=COST,
        name="forecast",
    )(*operands)


def analysis_kernel(state, mix, out, planes):
    pitch = ROWS + 1
    over_last = (((1,), (1,)), ((), ()))
    both = mix[...]

    def body(x, carry):
        s = state[0, 0, pl.ds(2 * x, 2)].reshape(2 * COLS, MEMBERS)
        mixed = lax.dot_general(
            both, jnp.concatenate([s, s], axis=1), over_last, preferred_element_type=F32
        )
        planes[pl.ds(2 * x, MEMBERS, stride=pitch), :] = mixed[:, :COLS]
        planes[pl.ds(2 * x + 1, MEMBERS, stride=pitch), :] = mixed[:, COLS:]
        return carry

    lax.fori_loop(0, ROWS // 2, body, 0, unroll=2)

    def gather(m, carry):
        for k in range(4):
            out[0, 0, 4 * m + k] = planes[pl.ds((4 * m + k) * pitch, ROWS), :].astype(BF16)
        return carry

    lax.fori_loop(0, MEMBERS // 4, gather, 0, unroll=2)


def analyse(state, mix):
    return pl.pallas_call(
        analysis_kernel,
        grid=(LAYERS, 3),
        in_specs=[
            pl.BlockSpec((1, 1, ROWS, COLS, MEMBERS), lambda i, j: (i, j, 0, 0, 0)),
            pl.BlockSpec((MEMBERS, 2 * MEMBERS), lambda i, j: (0, 0)),
        ],
        out_specs=pl.BlockSpec((1, 1, MEMBERS, ROWS, COLS), lambda i, j: (i, j, 0, 0, 0)),
        out_shape=jax.ShapeDtypeStruct((LAYERS, 3, MEMBERS, ROWS, COLS), BF16),
        scratch_shapes=[pltpu.VMEM((MEMBERS * (ROWS + 1), COLS), F32)],
        compiler_params=params(),
        cost_estimate=COST,
        name="analysis",
    )(state, mix)


def split3(x):
    a = lax.reduce_precision(x, 8, 7)
    b = lax.reduce_precision(x - a, 8, 7)
    c = lax.reduce_precision(x - a - b, 8, 7)
    return [p.astype(BF16) for p in (a, b, c)]


def observed_cells(dest, cell, value, sigma, with_last):
    tiles = lax.axis_size("gy")
    inverse = 1.0 / sigma
    weight = inverse * inverse
    pieces = jnp.stack(split3(weight) + split3(value * weight), 0).reshape(6, -1)
    row = ((dest ^ lax.axis_index("gy"))[:, None] * ROWS + cell // COLS).reshape(-1)
    col = (cell % COLS).reshape(-1)
    row_hot = (row[None, :] == jnp.arange(tiles * ROWS, dtype=jnp.int32)[:, None]).astype(BF16)
    col_hot = col[:, None] == jnp.arange(COLS, dtype=jnp.int32)[None, :]
    spread = jnp.where(col_hot[None], pieces[:, :, None], jnp.zeros((), BF16))
    field = jnp.einsum("rk,pkc->prc", row_hot, spread, preferred_element_type=F32)
    field = jnp.stack([field[2] + field[1] + field[0], field[5] + field[4] + field[3]], 0)
    field = field.reshape(2, tiles, ROWS, COLS).transpose(1, 0, 2, 3)
    bit = tiles // 2
    while bit:
        if bit == 1:
            field, with_last = lax.optimization_barrier((field, with_last))
        swap = [(i, i ^ bit) for i in range(tiles)]
        field = field[:bit] + lax.ppermute(field[bit:], "gy", swap)
        bit //= 2
    return field[0, 0], field[0, 1], with_last


def sum_everywhere(x):
    def other(axis, k):
        return lax.ppermute(x, axis, [(i, i ^ k) for i in range(lax.axis_size(axis))])

    x = x + other("gy", 1)
    for axis, unit in (("gy", 2), ("gx", 1), ("gx", 4)):
        x = (x + other(axis, unit)) + (other(axis, 2 * unit) + other(axis, 3 * unit))
    return x


def transform_kernel(total, mix, work, inverse):
    n = MEMBERS
    full = lax.Precision.HIGHEST
    rows_i = lax.broadcasted_iota(jnp.int32, (n, n), 0)
    cols_i = lax.broadcasted_iota(jnp.int32, (n, n), 1)
    eye = (rows_i == cols_i).astype(F32)
    work[:, 0:n] = total[0:n, :] + F32(n - 1) * eye
    work[:, n:2 * n] = eye
    sub = lax.broadcasted_iota(jnp.int32, (PANEL, n), 0)
    for first in range(0, n, PANEL):
        rows = slice(first, first + PANEL)
        up, inv = work[rows, 0:n], work[rows, n:2 * n]
        cols = [jnp.broadcast_to(up[:, first + k:first + k + 1], (PANEL, n)) for k in range(PANEL)]
        scale = jnp.zeros((PANEL, n), F32)
        for k in range(PANEL):
            pivot = cols[k][k:k + 1]
            scale = jnp.where(sub == k, pivot, scale)
            if k + 1 < PANEL:
                times = jnp.where(sub > k, cols[k], 0.0) * (1.0 / pivot)
                for q in range(k + 1, PANEL):
                    cols[q] = cols[q] - times * cols[q][k:k + 1]
                up = up - times * up[k:k + 1]
                inv = inv - times * inv[k:k + 1]
        scale = lax.rsqrt(scale)
        up, inv = up * scale, inv * scale
        inverse[rows, :] = inv
        after = first + PANEL
        if after < n:
            update = lax.dot_general(
                up, jnp.concatenate([up, inv], axis=1), (((0,), (0,)), ((), ())),
                precision=full, preferred_element_type=F32,
            )
            work[after:, :] = work[after:, :] - update[after:, :]
    low = inverse[...]
    proj = total[n:n + 8, :]
    inner = lax.dot_general(proj, low, (((1,), (1,)), ((), ())), precision=full, preferred_element_type=F32)
    weights = jnp.dot(inner, low, precision=full, preferred_element_type=F32)
    transform_t = weights[0:1] + F32((n - 1) ** 0.5) * low
    spare = (1.0 - jnp.sum(transform_t, axis=1, keepdims=True)) * (1.0 / n)
    value = transform_t + spare
    high = value.astype(BF16)
    mix[:, 0:n] = high
    mix[:, n:2 * n] = (value - high.astype(F32)).astype(BF16)


def make_mix(total):
    vmem = pl.BlockSpec(memory_space=pltpu.VMEM)
    return pl.pallas_call(
        transform_kernel,
        in_specs=[vmem],
        out_specs=vmem,
        out_shape=jax.ShapeDtypeStruct((MEMBERS, 2 * MEMBERS), BF16),
        scratch_shapes=[
            pltpu.VMEM((MEMBERS, 2 * MEMBERS), F32),
            pltpu.VMEM((MEMBERS, MEMBERS), F32),
        ],
        compiler_params=params(),
        cost_estimate=COST,
        name="transform",
    )(total)


def on_device(ensemble, layer_depth, obs_dest, obs_cell, obs_value, obs_sigma):
    row0 = lax.axis_index("gx") * ROWS - HALO + jnp.arange(WIDE_ROWS, dtype=jnp.int32)
    col0 = lax.axis_index("gy") * COLS - HALO + jnp.arange(COLS + 2 * HALO, dtype=jnp.int32)
    row_in = (row0 >= 0) & (row0 < lax.axis_size("gx") * ROWS)
    col_in = (col0 >= 0) & (col0 < lax.axis_size("gy") * COLS)
    d = layer_depth
    d = jnp.concatenate(
        [shift(d[:, ROWS - HALO:], "gx", 1), d, shift(d[:, :HALO], "gx", -1)], axis=1
    )
    own, left_out, right_out, north, south = all_rows(ensemble)
    observed = (obs_dest[0, 0], obs_cell[0, 0], obs_value[0, 0], obs_sigma[0, 0])
    d, north, south = lax.optimization_barrier((d, north, south))
    top = shift(south, "gx", 1)
    bottom = shift(north, "gx", -1)
    left = shift(right_out, "gy", 1)
    right = shift(left_out, "gy", -1)
    d, left, observed = lax.optimization_barrier((d, left, observed))
    d = jnp.concatenate(
        [shift(d[:, :, COLS - HALO:], "gy", 1), d, shift(d[:, :, :HALO], "gy", -1)], axis=2
    )
    d = jnp.where(row_in[:, None] & col_in[None, :], (HALF * HALF) * d, 0.0).astype(BF16)
    d = d.reshape(LAYERS, WIDE_ROWS, SEGMENTS, POSITIONS).transpose(0, 1, 3, 2)
    depth = jnp.broadcast_to(d[..., None], d.shape + (MEMBERS,))
    mask = col_in.reshape(SEGMENTS, POSITIONS).T.astype(BF16)
    mask = jnp.stack([jnp.zeros_like(mask), mask], axis=0)
    masks = jnp.broadcast_to(mask[..., None], mask.shape + (MEMBERS,))
    row_in = row_in.astype(jnp.int32)[None, :]
    sides = jnp.stack([left, right], axis=0)
    corner_t = shift(sides[:, :, :, 12:], "gx", 1)
    corner_b = shift(sides[:, :, :, :4], "gx", -1)

    weight, pull, (depth, masks) = observed_cells(*observed, (depth, masks))
    state, total = forecast(
        own, top, bottom, left, right, corner_t, corner_b, depth, row_in, masks, weight, pull
    )
    total = sum_everywhere(total)
    return analyse(state, make_mix(total))


def solution(mesh):
    in_specs = (
        P(None, None, None, "gx", "gy"),
        P(None, "gx", "gy"),
        P("gx", "gy", None),
        P("gx", "gy", None, None),
        P("gx", "gy", None, None),
        P("gx", "gy", None, None),
    )
    out_specs = P(None, None, None, "gx", "gy")
    return jax.shard_map(
        on_device, mesh=mesh, in_specs=in_specs, out_specs=out_specs, check_vma=False
    )
```

```python
import jax
import jax.numpy as jnp
from jax import lax
from jax.experimental import pallas as pl
from jax.experimental.pallas import tpu as pltpu
from jax.sharding import PartitionSpec as P

MEMBERS = 128
ROWS = 32
COLS = 128
HALO = 8
STEPS = 4
WIDE_ROWS = ROWS + 2 * HALO
WIDE_COLS = COLS + 2 * HALO
SEGMENTS = 16
POSITIONS = WIDE_COLS // SEGMENTS
LINE = 40
PANEL = 32
LAYERS = 2
HALF = 0.15
TURN = 0.12
COUPLING = 0.5

F32 = jnp.float32
BF16 = jnp.bfloat16


COST = pl.CostEstimate(flops=1, bytes_accessed=1, transcendentals=0)


def params(mib):
    return pltpu.CompilerParams(vmem_limit_bytes=mib * 1024 * 1024)


def shift(x, axis, by):
    n = lax.axis_size(axis)
    return lax.ppermute(x, axis, [(i, (i + by) % n) for i in range(n)])


def turn_rows(e_ref, planes, rows, put):
    pitch = ROWS + 1
    tiles = sorted({x // 8 * 8 for x in rows})

    def spread(m, carry):
        for k in range(4):
            plane = e_ref[0, 0, 4 * m + k].astype(F32)
            for lo in tiles:
                planes[pl.ds((4 * m + k) * pitch + lo, 8), :] = plane[lo:lo + 8]
        return carry

    lax.fori_loop(0, MEMBERS // 4, spread, 0, unroll=8)
    for x in rows:
        put(x, planes[pl.ds(x, MEMBERS, stride=pitch), :].astype(BF16).T)


E_BLOCK = pl.BlockSpec((1, 1, MEMBERS, ROWS, COLS), lambda i, j: (i, j, 0, 0, 0))
FAR = 3 * HALO - 2


def all_rows(ensemble):
    def kernel(e_ref, own, left, right, north, south, planes):
        part = pl.program_id(1)
        base = pl.program_id(0) * FAR + part * (HALO - 1) + (part > 0)
        held = {}

        def put(x, value):
            own[0, 0, x] = value
            if x % 2:
                other = held.pop(x - 1)
                left[0, 0, x // 2] = jnp.concatenate([other[:HALO], value[:HALO]], axis=0)
                right[0, 0, x // 2] = jnp.concatenate(
                    [other[COLS - HALO:], value[COLS - HALO:]], axis=0
                )
            else:
                held[x] = value
            if x < HALO - 1:
                north[base + x] = value
            elif x > ROWS - HALO:
                south[base + (x - (ROWS - HALO)) - (part > 0)] = value
            elif x == HALO - 1:

                @pl.when(part == 0)
                def _():
                    north[base + x] = value

            elif x == ROWS - HALO:

                @pl.when(part == 0)
                def _():
                    south[base] = value

        turn_rows(e_ref, planes, list(range(ROWS)), put)

    def whole(block):
        return jax.ShapeDtypeStruct((LAYERS, 3) + block[2:], BF16)

    def spec(block):
        return pl.BlockSpec(block, lambda i, j: (i, j, 0, 0, 0))

    tile = (1, 1, ROWS, COLS, MEMBERS)
    side = (1, 1, ROWS // 2, 16, MEMBERS)
    edge = (LAYERS * FAR, COLS, MEMBERS)
    edge_spec = pl.BlockSpec(edge, lambda i, j: (0, 0, 0))
    edge_shape = jax.ShapeDtypeStruct(edge, BF16)
    return pl.pallas_call(
        kernel,
        grid=(LAYERS, 3),
        in_specs=[E_BLOCK],
        out_specs=[spec(tile), spec(side), spec(side), edge_spec, edge_spec],
        out_shape=[whole(tile), whole(side), whole(side), edge_shape, edge_shape],
        scratch_shapes=[pltpu.VMEM((MEMBERS * (ROWS + 1), COLS), F32)],
        compiler_params=params(18),
        cost_estimate=COST,
        name="all_rows",
    )(ensemble)


def forecast_kernel(
    own, top, bottom, left, right, corner_t, corner_b, depth_in, row_in, masks, weight, pull,
    out, total, raw, raw_side, depth, st, fx, fy, pr, line, y_parts, z_parts, acc, sems,
):
    depth_copy = pltpu.make_async_copy(depth_in, depth, sems.at[54])
    depth_copy.start()
    order = [(l, c) for l in range(LAYERS) for c in range(3)]
    copies = {}
    for l, c in order:
        count = HALO - (c > 0)
        at = pl.ds(l * FAR + c * (HALO - 1) + (c > 0), count)
        rows = [
            (own.at[l, c], raw.at[l, c, pl.ds(HALO, ROWS)]),
            (top.at[at], raw.at[l, c, pl.ds(HALO - count, count)]),
            (bottom.at[at], raw.at[l, c, pl.ds(HALO + ROWS, count)]),
        ]
        for k, piece in enumerate((left, right)):
            rows.append((piece.at[l, c], raw_side.at[k, l, c, pl.ds(4, 16)]))
            rows.append((corner_t.at[k, l, c], raw_side.at[k, l, c, pl.ds(0, 4)]))
            rows.append((corner_b.at[k, l, c], raw_side.at[k, l, c, pl.ds(20, 4)]))
        copies[l, c] = [
            pltpu.make_async_copy(x, y, sems.at[(3 * l + c) * 9 + k])
            for k, (x, y) in enumerate(rows)
        ]
    for key in order:
        for c in copies[key]:
            c.start()
    depth_copy.wait()

    def rolled(x, by):
        return pltpu.roll(x.astype(F32), by % SEGMENTS, 0).astype(BF16)

    def put_flux(l, r, flux):
        fy[l, r, 1:POSITIONS + 1] = flux
        fy[l, r, 0] = rolled(flux[POSITIONS - 1], 1)
        fy[l, r, POSITIONS + 1] = rolled(flux[0], -1)

    def put_pressure(l, r, value):
        pr[l, r, 1:POSITIONS + 1] = value
        pr[l, r, 0] = rolled(value[POSITIONS - 1], 1)
        pr[l, r, POSITIONS + 1] = rolled(value[0], -1)

    for l, c in order:
        for d in copies[l, c]:
            d.wait()

        def unpack(pair, carry):
            scale = HALF if c == 2 else 1.0
            sides = [raw_side[k, l, c, pair].astype(F32) * scale for k in range(2)]
            for odd in range(2):
                r = 2 * pair + odd
                base = lax.rem(pair, 2) * (8 * LINE) + odd * (4 * LINE)
                half = slice(8 * odd, 8 * odd + 8)
                line[pl.ds(base, 8), :] = sides[0][half]
                line[pl.ds(base + 8, COLS), :] = raw[l, c, r].astype(F32) * scale
                line[pl.ds(base + 8 + COLS, 8), :] = sides[1][half]
                value = jnp.stack(
                    [
                        line[pl.ds(base + p, SEGMENTS, stride=POSITIONS), :].astype(BF16)
                        for p in range(POSITIONS)
                    ],
                    axis=0,
                )
                st[l, c, r] = value
                if c == 0:
                    fx[l, r] = depth[l, r] * value
                elif c == 1:
                    put_flux(l, r, depth[l, r] * value)
            return carry

        lax.fori_loop(0, WIDE_ROWS // 2, unpack, 0, unroll=2)

    mid = slice(1, POSITIONS + 1)

    def sweep(body, rows_from, rows_to, first):
        for start in (rows_from, rows_from + 1):
            lax.fori_loop(
                0,
                (rows_to - rows_from) // 2,
                lambda i, above, start=start: body(start + 2 * i, above),
                first(start),
                unroll=2,
            )

    for step in range(1, STEPS + 1):

        def thickness(r, above):
            new, below = [], []
            for l in range(LAYERS):
                nxt = fx[l, r + 1]
                g = fy[l, r]
                h = st[l, 2, r] - ((nxt - above[l]) + (g[2:] - g[:POSITIONS]))
                st[l, 2, r] = h
                new.append(h)
                below.append(nxt)
            mask = masks[row_in[0, r]]
            put_pressure(0, r, (new[0] + new[1]) * mask)
            put_pressure(1, r, (BF16(COUPLING) * new[0] + new[1]) * mask)
            return tuple(below)

        sweep(
            thickness, 2 * step - 1, WIDE_ROWS - (2 * step - 1),
            lambda r: tuple(fx[l, r - 1] for l in range(LAYERS)),
        )

        def velocity(r, above):
            below = []
            for l in range(LAYERS):
                u, v = st[l, 0, r], st[l, 1, r]
                nxt = pr[l, r + 1, mid]
                g = pr[l, r]
                u_new = (u + BF16(TURN) * v) - (nxt - above[l])
                v_new = (v - BF16(TURN) * u) - (g[2:] - g[:POSITIONS])
                st[l, 0, r] = u_new
                st[l, 1, r] = v_new
                if step < STEPS:
                    d = depth[l, r]
                    fx[l, r] = d * u_new
                    put_flux(l, r, d * v_new)
                below.append(nxt)
            return tuple(below)

        sweep(
            velocity, 2 * step, WIDE_ROWS - 2 * step,
            lambda r: tuple(pr[l, r - 1, mid] for l in range(LAYERS)),
        )

    done = []
    for c in (2, 0, 1):
        for l in range(LAYERS):

            def pack(r, carry):
                base = lax.rem(r, 4) * (4 * LINE)
                for p in range(POSITIONS):
                    line[pl.ds(base + p, SEGMENTS, stride=POSITIONS), :] = st[
                        l, c, r + HALO, p
                    ].astype(F32)
                value = line[pl.ds(base + 8, COLS), :]
                if c == 2:
                    value = value * (1.0 / HALF)
                raw[l, c, r] = value.astype(BF16)
                return carry

            lax.fori_loop(0, ROWS, pack, 0, unroll=4)
            done.append(
                pltpu.make_async_copy(
                    raw.at[l, c, pl.ds(0, ROWS)], out.at[l, c], sems.at[55 + 3 * l + c]
                )
            )
            done[-1].start()
    add_up(raw, weight, pull, total, y_parts, z_parts, acc)
    for d in done:
        d.wait()


def add_up(state, weight, pull, total, left, right, acc):
    n = MEMBERS
    over_last = (((1,), (1,)), ((), ()))
    eye = lax.broadcasted_iota(jnp.int32, (n, n), 0) == lax.broadcasted_iota(jnp.int32, (n, n), 1)
    away = (eye.astype(F32) - 1.0 / n).astype(BF16)
    away = jnp.concatenate([away, away], axis=1)
    share = jnp.full((8, 2 * n), 1.0 / n, BF16)
    acc[...] = jnp.zeros_like(acc)

    def body(x, carry):
        both = jnp.concatenate([state[0, 2, x], state[1, 2, x]], axis=1)
        z = lax.dot_general(both, away, over_last, preferred_element_type=F32)
        zt = lax.dot_general(away, both, over_last, preferred_element_type=F32)
        mean = lax.dot_general(share, both, over_last, preferred_element_type=F32)[0:1]
        w = weight[pl.ds(x, 1), :]
        y = zt * w
        y_high = y.astype(BF16)
        z_high = z.astype(BF16)
        left[0, x] = y_high
        left[1, x] = (y - y_high.astype(F32)).astype(BF16)
        right[x, :, 0:n] = z_high
        right[x, :, n:2 * n] = (z - z_high.astype(F32)).astype(BF16)
        acc[...] += zt * (pull[pl.ds(x, 1), :] - mean * w)
        return carry

    lax.fori_loop(0, ROWS, body, 0, unroll=8)

    def multiply(x, part):
        a = jnp.concatenate([left[0, 2 * x], left[0, 2 * x + 1]], axis=1)
        b = jnp.concatenate([left[1, 2 * x], left[1, 2 * x + 1]], axis=1)
        z = right[pl.ds(2 * x, 2)].reshape(2 * COLS, 2 * n)
        main = jnp.dot(a, z, preferred_element_type=F32)
        low = jnp.dot(b, z[:, 0:n], preferred_element_type=F32)
        return part + (main[:, 0:n] + (main[:, n:2 * n] + low))

    total[0:n, :] = lax.fori_loop(0, ROWS // 2, multiply, jnp.zeros((n, n), F32), unroll=8)
    total[n:n + 8, :] = jnp.broadcast_to(jnp.sum(acc[...].T, axis=0, keepdims=True), (8, n))


def forecast(*operands):
    plane = (LAYERS, WIDE_ROWS, POSITIONS, SEGMENTS, MEMBERS)
    padded = (LAYERS, WIDE_ROWS, POSITIONS + 2, SEGMENTS, MEMBERS)
    anywhere = pl.BlockSpec(memory_space=pl.ANY)
    vmem = pl.BlockSpec(memory_space=pltpu.VMEM)
    return pl.pallas_call(
        forecast_kernel,
        in_specs=[anywhere] * 8 + [pl.BlockSpec(memory_space=pltpu.SMEM), vmem, vmem, vmem],
        out_specs=[anywhere, vmem],
        out_shape=[
            jax.ShapeDtypeStruct((LAYERS, 3, ROWS, COLS, MEMBERS), BF16),
            jax.ShapeDtypeStruct((MEMBERS + 8, MEMBERS), F32),
        ],
        scratch_shapes=[
            pltpu.VMEM((LAYERS, 3, WIDE_ROWS, COLS, MEMBERS), BF16),
            pltpu.VMEM((2, LAYERS, 3, WIDE_ROWS // 2, 16, MEMBERS), BF16),
            pltpu.VMEM(plane, BF16),
            pltpu.VMEM((LAYERS, 3) + plane[1:], BF16),
            pltpu.VMEM(plane, BF16),
            pltpu.VMEM(padded, BF16),
            pltpu.VMEM(padded, BF16),
            pltpu.VMEM((16 * LINE, MEMBERS), F32),
            pltpu.VMEM((2, ROWS, MEMBERS, COLS), BF16),
            pltpu.VMEM((ROWS, COLS, 2 * MEMBERS), BF16),
            pltpu.VMEM((MEMBERS, COLS), F32),
            pltpu.SemaphoreType.DMA((61,)),
        ],
        compiler_params=params(47),
        cost_estimate=COST,
        name="forecast",
    )(*operands)


def analysis_kernel(state, mix, out, planes):
    pitch = ROWS + 1
    over_last = (((1,), (1,)), ((), ()))
    both = mix[...]

    def body(x, carry):
        s = state[0, 0, pl.ds(2 * x, 2)].reshape(2 * COLS, MEMBERS)
        mixed = lax.dot_general(
            both, jnp.concatenate([s, s], axis=1), over_last, preferred_element_type=F32
        )
        planes[pl.ds(2 * x, MEMBERS, stride=pitch), :] = mixed[:, :COLS]
        planes[pl.ds(2 * x + 1, MEMBERS, stride=pitch), :] = mixed[:, COLS:]
        return carry

    lax.fori_loop(0, ROWS // 2, body, 0, unroll=16)

    def gather(m, carry):
        for k in range(4):
            out[0, 0, 4 * m + k] = planes[pl.ds((4 * m + k) * pitch, ROWS), :].astype(BF16)
        return carry

    lax.fori_loop(0, MEMBERS // 4, gather, 0, unroll=16)


def analyse(state, mix):
    return pl.pallas_call(
        analysis_kernel,
        grid=(LAYERS, 3),
        in_specs=[
            pl.BlockSpec((1, 1, ROWS, COLS, MEMBERS), lambda i, j: (i, j, 0, 0, 0)),
            pl.BlockSpec((MEMBERS, 2 * MEMBERS), lambda i, j: (0, 0)),
        ],
        out_specs=pl.BlockSpec((1, 1, MEMBERS, ROWS, COLS), lambda i, j: (i, j, 0, 0, 0)),
        out_shape=jax.ShapeDtypeStruct((LAYERS, 3, MEMBERS, ROWS, COLS), BF16),
        scratch_shapes=[pltpu.VMEM((MEMBERS * (ROWS + 1), COLS), F32)],
        compiler_params=params(14),
        cost_estimate=COST,
        name="analysis",
    )(state, mix)


def split3(x):
    a = lax.reduce_precision(x, 8, 7)
    b = lax.reduce_precision(x - a, 8, 7)
    c = lax.reduce_precision(x - a - b, 8, 7)
    return [p.astype(BF16) for p in (a, b, c)]


def observed_cells(dest, cell, value, sigma, with_last):
    tiles = lax.axis_size("gy")
    inverse = 1.0 / sigma
    weight = inverse * inverse
    pieces = jnp.stack(split3(weight) + split3(value * weight), 0).reshape(6, -1)
    row = ((dest ^ lax.axis_index("gy"))[:, None] * ROWS + cell // COLS).reshape(-1)
    col = (cell % COLS).reshape(-1)
    row_hot = (row[None, :] == jnp.arange(tiles * ROWS, dtype=jnp.int32)[:, None]).astype(BF16)
    col_hot = col[:, None] == jnp.arange(COLS, dtype=jnp.int32)[None, :]
    spread = jnp.where(col_hot[None], pieces[:, :, None], jnp.zeros((), BF16))
    field = jnp.einsum("rk,pkc->prc", row_hot, spread, preferred_element_type=F32)
    field = jnp.stack([field[2] + field[1] + field[0], field[5] + field[4] + field[3]], 0)
    field = field.reshape(2, tiles, ROWS, COLS).transpose(1, 0, 2, 3)
    bit = tiles // 2
    while bit:
        if bit == 1:
            field, with_last = lax.optimization_barrier((field, with_last))
        swap = [(i, i ^ bit) for i in range(tiles)]
        field = field[:bit] + lax.ppermute(field[bit:], "gy", swap)
        bit //= 2
    return field[0, 0], field[0, 1], with_last


def sum_everywhere(x):
    def other(axis, k):
        return lax.ppermute(x, axis, [(i, i ^ k) for i in range(lax.axis_size(axis))])

    x = x + other("gy", 1)
    for axis, unit in (("gy", 2), ("gx", 1), ("gx", 4)):
        x = (x + other(axis, unit)) + (other(axis, 2 * unit) + other(axis, 3 * unit))
    return x


def transform_kernel(total, mix, work, inverse):
    n = MEMBERS
    full = lax.Precision.HIGHEST
    rows_i = lax.broadcasted_iota(jnp.int32, (n, n), 0)
    cols_i = lax.broadcasted_iota(jnp.int32, (n, n), 1)
    eye = (rows_i == cols_i).astype(F32)
    work[:, 0:n] = total[0:n, :] + F32(n - 1) * eye
    work[:, n:2 * n] = eye
    sub = lax.broadcasted_iota(jnp.int32, (PANEL, n), 0)
    for first in range(0, n, PANEL):
        rows = slice(first, first + PANEL)
        up, inv = work[rows, 0:n], work[rows, n:2 * n]
        cols = [jnp.broadcast_to(up[:, first + k:first + k + 1], (PANEL, n)) for k in range(PANEL)]
        scale = jnp.zeros((PANEL, n), F32)
        for k in range(PANEL):
            pivot = cols[k][k:k + 1]
            scale = jnp.where(sub == k, pivot, scale)
            if k + 1 < PANEL:
                times = jnp.where(sub > k, cols[k], 0.0) * (1.0 / pivot)
                for q in range(k + 1, PANEL):
                    cols[q] = cols[q] - times * cols[q][k:k + 1]
                up = up - times * up[k:k + 1]
                inv = inv - times * inv[k:k + 1]
        scale = lax.rsqrt(scale)
        up, inv = up * scale, inv * scale
        inverse[rows, :] = inv
        after = first + PANEL
        if after < n:
            update = lax.dot_general(
                up, jnp.concatenate([up, inv], axis=1), (((0,), (0,)), ((), ())),
                precision=full, preferred_element_type=F32,
            )
            work[after:, :] = work[after:, :] - update[after:, :]
    low = inverse[...]
    proj = total[n:n + 8, :]
    inner = lax.dot_general(proj, low, (((1,), (1,)), ((), ())), precision=full, preferred_element_type=F32)
    weights = jnp.dot(inner, low, precision=full, preferred_element_type=F32)
    transform_t = weights[0:1] + F32((n - 1) ** 0.5) * low
    spare = (1.0 - jnp.sum(transform_t, axis=1, keepdims=True)) * (1.0 / n)
    value = transform_t + spare
    high = value.astype(BF16)
    mix[:, 0:n] = high
    mix[:, n:2 * n] = (value - high.astype(F32)).astype(BF16)


def make_mix(total):
    vmem = pl.BlockSpec(memory_space=pltpu.VMEM)
    return pl.pallas_call(
        transform_kernel,
        in_specs=[vmem],
        out_specs=vmem,
        out_shape=jax.ShapeDtypeStruct((MEMBERS, 2 * MEMBERS), BF16),
        scratch_shapes=[
            pltpu.VMEM((MEMBERS, 2 * MEMBERS), F32),
            pltpu.VMEM((MEMBERS, MEMBERS), F32),
        ],
        compiler_params=params(8),
        cost_estimate=COST,
        name="transform",
    )(total)


def on_device(ensemble, layer_depth, obs_dest, obs_cell, obs_value, obs_sigma):
    row0 = lax.axis_index("gx") * ROWS - HALO + jnp.arange(WIDE_ROWS, dtype=jnp.int32)
    col0 = lax.axis_index("gy") * COLS - HALO + jnp.arange(COLS + 2 * HALO, dtype=jnp.int32)
    row_in = (row0 >= 0) & (row0 < lax.axis_size("gx") * ROWS)
    col_in = (col0 >= 0) & (col0 < lax.axis_size("gy") * COLS)
    d = layer_depth
    d = jnp.concatenate(
        [shift(d[:, ROWS - HALO:], "gx", 1), d, shift(d[:, :HALO], "gx", -1)], axis=1
    )
    own, left_out, right_out, north, south = all_rows(ensemble)
    observed = (obs_dest[0, 0], obs_cell[0, 0], obs_value[0, 0], obs_sigma[0, 0])
    d, north, south = lax.optimization_barrier((d, north, south))
    top = shift(south, "gx", 1)
    bottom = shift(north, "gx", -1)
    left = shift(right_out, "gy", 1)
    right = shift(left_out, "gy", -1)
    d, left, observed = lax.optimization_barrier((d, left, observed))
    d = jnp.concatenate(
        [shift(d[:, :, COLS - HALO:], "gy", 1), d, shift(d[:, :, :HALO], "gy", -1)], axis=2
    )
    d = jnp.where(row_in[:, None] & col_in[None, :], (HALF * HALF) * d, 0.0).astype(BF16)
    d = d.reshape(LAYERS, WIDE_ROWS, SEGMENTS, POSITIONS).transpose(0, 1, 3, 2)
    depth = jnp.broadcast_to(d[..., None], d.shape + (MEMBERS,))
    mask = col_in.reshape(SEGMENTS, POSITIONS).T.astype(BF16)
    mask = jnp.stack([jnp.zeros_like(mask), mask], axis=0)
    masks = jnp.broadcast_to(mask[..., None], mask.shape + (MEMBERS,))
    row_in = row_in.astype(jnp.int32)[None, :]
    sides = jnp.stack([left, right], axis=0)
    corner_t = shift(sides[:, :, :, 12:], "gx", 1)
    corner_b = shift(sides[:, :, :, :4], "gx", -1)

    weight, pull, (depth, masks) = observed_cells(*observed, (depth, masks))
    state, total = forecast(
        own, top, bottom, left, right, corner_t, corner_b, depth, row_in, masks, weight, pull
    )
    total = sum_everywhere(total)
    return analyse(state, make_mix(total))


def solution(mesh):
    in_specs = (
        P(None, None, None, "gx", "gy"),
        P(None, "gx", "gy"),
        P("gx", "gy", None),
        P("gx", "gy", None, None),
        P("gx", "gy", None, None),
        P("gx", "gy", None, None),
    )
    out_specs = P(None, None, None, "gx", "gy")
    return jax.shard_map(
        on_device, mesh=mesh, in_specs=in_specs, out_specs=out_specs, check_vma=False
    )
```

```python
import jax
import jax.numpy as jnp
from jax import lax
from jax.experimental import pallas as pl
from jax.experimental.pallas import tpu as pltpu
from jax.sharding import PartitionSpec as P

MEMBERS = 128
ROWS = 32
COLS = 128
HALO = 8
STEPS = 4
WIDE_ROWS = ROWS + 2 * HALO
WIDE_COLS = COLS + 2 * HALO
SEGMENTS = 16
POSITIONS = WIDE_COLS // SEGMENTS
LINE = 40
PANEL = 32
LAYERS = 2
HALF = 0.15
TURN = 0.12
COUPLING = 0.5

F32 = jnp.float32
BF16 = jnp.bfloat16


COST = pl.CostEstimate(flops=1, bytes_accessed=1, transcendentals=0)


def params(mib):
    return pltpu.CompilerParams(vmem_limit_bytes=mib * 1024 * 1024)


def shift(x, axis, by):
    n = lax.axis_size(axis)
    return lax.ppermute(x, axis, [(i, (i + by) % n) for i in range(n)])


def turn_rows(e_ref, planes, rows, put):
    pitch = ROWS + 1
    tiles = sorted({x // 8 * 8 for x in rows})

    def spread(m, carry):
        for k in range(4):
            plane = e_ref[0, 0, 4 * m + k].astype(F32)
            for lo in tiles:
                planes[pl.ds((4 * m + k) * pitch + lo, 8), :] = plane[lo:lo + 8]
        return carry

    lax.fori_loop(0, MEMBERS // 4, spread, 0, unroll=8)
    for x in rows:
        put(x, planes[pl.ds(x, MEMBERS, stride=pitch), :].astype(BF16).T)


E_BLOCK = pl.BlockSpec((1, 1, MEMBERS, ROWS, COLS), lambda i, j: (i, j, 0, 0, 0))
FAR = 3 * HALO - 2


def all_rows(ensemble):
    def kernel(e_ref, own, left, right, north, south, planes):
        part = pl.program_id(1)
        base = pl.program_id(0) * FAR + part * (HALO - 1) + (part > 0)
        held = {}

        def put(x, value):
            own[0, 0, x] = value
            if x % 2:
                other = held.pop(x - 1)
                left[0, 0, x // 2] = jnp.concatenate([other[:HALO], value[:HALO]], axis=0)
                right[0, 0, x // 2] = jnp.concatenate(
                    [other[COLS - HALO:], value[COLS - HALO:]], axis=0
                )
            else:
                held[x] = value
            if x < HALO - 1:
                north[base + x] = value
            elif x > ROWS - HALO:
                south[base + (x - (ROWS - HALO)) - (part > 0)] = value
            elif x == HALO - 1:

                @pl.when(part == 0)
                def _():
                    north[base + x] = value

            elif x == ROWS - HALO:

                @pl.when(part == 0)
                def _():
                    south[base] = value

        turn_rows(e_ref, planes, list(range(ROWS)), put)

    def whole(block):
        return jax.ShapeDtypeStruct((LAYERS, 3) + block[2:], BF16)

    def spec(block):
        return pl.BlockSpec(block, lambda i, j: (i, j, 0, 0, 0))

    tile = (1, 1, ROWS, COLS, MEMBERS)
    side = (1, 1, ROWS // 2, 16, MEMBERS)
    edge = (LAYERS * FAR, COLS, MEMBERS)
    edge_spec = pl.BlockSpec(edge, lambda i, j: (0, 0, 0))
    edge_shape = jax.ShapeDtypeStruct(edge, BF16)
    return pl.pallas_call(
        kernel,
        grid=(LAYERS, 3),
        in_specs=[E_BLOCK],
        out_specs=[spec(tile), spec(side), spec(side), edge_spec, edge_spec],
        out_shape=[whole(tile), whole(side), whole(side), edge_shape, edge_shape],
        scratch_shapes=[pltpu.VMEM((MEMBERS * (ROWS + 1), COLS), F32)],
        compiler_params=params(60),
        cost_estimate=COST,
        name="all_rows",
    )(ensemble)


def forecast_kernel(
    own, top, bottom, left, right, corner_t, corner_b, depth, row_in, masks, weight, pull,
    out, total, raw, raw_side, st, fx, fy, pr, line, y_parts, z_parts, acc, sems,
):
    order = [(l, c) for l in range(LAYERS) for c in range(3)]
    copies = {}
    for l, c in order:
        count = HALO - (c > 0)
        at = pl.ds(l * FAR + c * (HALO - 1) + (c > 0), count)
        rows = [
            (own.at[l, c], raw.at[l, c, pl.ds(HALO, ROWS)]),
            (top.at[at], raw.at[l, c, pl.ds(HALO - count, count)]),
            (bottom.at[at], raw.at[l, c, pl.ds(HALO + ROWS, count)]),
        ]
        for k, piece in enumerate((left, right)):
            rows.append((piece.at[l, c], raw_side.at[k, l, c, pl.ds(4, 16)]))
            rows.append((corner_t.at[k, l, c], raw_side.at[k, l, c, pl.ds(0, 4)]))
            rows.append((corner_b.at[k, l, c], raw_side.at[k, l, c, pl.ds(20, 4)]))
        copies[l, c] = [
            pltpu.make_async_copy(x, y, sems.at[(3 * l + c) * 9 + k])
            for k, (x, y) in enumerate(rows)
        ]
    for key in order:
        for c in copies[key]:
            c.start()

    def rolled(x, by):
        return pltpu.roll(x.astype(F32), by % SEGMENTS, 0).astype(BF16)

    def put_flux(l, r, flux):
        fy[l, r, 1:POSITIONS + 1] = flux
        fy[l, r, 0] = rolled(flux[POSITIONS - 1], 1)
        fy[l, r, POSITIONS + 1] = rolled(flux[0], -1)

    def put_pressure(l, r, value):
        pr[l, r, 1:POSITIONS + 1] = value
        pr[l, r, 0] = rolled(value[POSITIONS - 1], 1)
        pr[l, r, POSITIONS + 1] = rolled(value[0], -1)

    for l, c in order:
        for d in copies[l, c]:
            d.wait()

        def unpack(pair, carry):
            scale = HALF if c == 2 else 1.0
            sides = [raw_side[k, l, c, pair].astype(F32) * scale for k in range(2)]
            for odd in range(2):
                r = 2 * pair + odd
                base = lax.rem(pair, 2) * (8 * LINE) + odd * (4 * LINE)
                half = slice(8 * odd, 8 * odd + 8)
                line[pl.ds(base, 8), :] = sides[0][half]
                line[pl.ds(base + 8, COLS), :] = raw[l, c, r].astype(F32) * scale
                line[pl.ds(base + 8 + COLS, 8), :] = sides[1][half]
                value = jnp.stack(
                    [
                        line[pl.ds(base + p, SEGMENTS, stride=POSITIONS), :].astype(BF16)
                        for p in range(POSITIONS)
                    ],
                    axis=0,
                )
                st[l, c, r] = value
                if c == 0:
                    fx[l, r] = depth[l, r] * value
                elif c == 1:
                    put_flux(l, r, depth[l, r] * value)
            return carry

        lax.fori_loop(0, WIDE_ROWS // 2, unpack, 0, unroll=2)

    mid = slice(1, POSITIONS + 1)

    def sweep(body, rows_from, rows_to, first):
        for start in (rows_from, rows_from + 1):
            lax.fori_loop(
                0,
                (rows_to - rows_from) // 2,
                lambda i, above, start=start: body(start + 2 * i, above),
                first(start),
                unroll=2,
            )

    for step in range(1, STEPS + 1):

        def thickness(r, above):
            new, below = [], []
            for l in range(LAYERS):
                nxt = fx[l, r + 1]
                g = fy[l, r]
                h = st[l, 2, r] - ((nxt - above[l]) + (g[2:] - g[:POSITIONS]))
                st[l, 2, r] = h
                new.append(h)
                below.append(nxt)
            mask = masks[row_in[0, r]]
            put_pressure(0, r, (new[0] + new[1]) * mask)
            put_pressure(1, r, (BF16(COUPLING) * new[0] + new[1]) * mask)
            return tuple(below)

        sweep(
            thickness, 2 * step - 1, WIDE_ROWS - (2 * step - 1),
            lambda r: tuple(fx[l, r - 1] for l in range(LAYERS)),
        )

        def velocity(r, above):
            below = []
            for l in range(LAYERS):
                u, v = st[l, 0, r], st[l, 1, r]
                nxt = pr[l, r + 1, mid]
                g = pr[l, r]
                u_new = (u + BF16(TURN) * v) - (nxt - above[l])
                v_new = (v - BF16(TURN) * u) - (g[2:] - g[:POSITIONS])
                st[l, 0, r] = u_new
                st[l, 1, r] = v_new
                if step < STEPS:
                    d = depth[l, r]
                    fx[l, r] = d * u_new
                    put_flux(l, r, d * v_new)
                below.append(nxt)
            return tuple(below)

        sweep(
            velocity, 2 * step, WIDE_ROWS - 2 * step,
            lambda r: tuple(pr[l, r - 1, mid] for l in range(LAYERS)),
        )

    done = []
    for c in (2, 0, 1):
        for l in range(LAYERS):

            def pack(r, carry):
                base = lax.rem(r, 4) * (4 * LINE)
                for p in range(POSITIONS):
                    line[pl.ds(base + p, SEGMENTS, stride=POSITIONS), :] = st[
                        l, c, r + HALO, p
                    ].astype(F32)
                value = line[pl.ds(base + 8, COLS), :]
                if c == 2:
                    value = value * (1.0 / HALF)
                raw[l, c, r] = value.astype(BF16)
                return carry

            lax.fori_loop(0, ROWS, pack, 0, unroll=4)
            done.append(
                pltpu.make_async_copy(
                    raw.at[l, c, pl.ds(0, ROWS)], out.at[l, c], sems.at[54 + 3 * l + c]
                )
            )
            done[-1].start()
    add_up(raw, weight, pull, total, y_parts, z_parts, acc)
    for d in done:
        d.wait()


def add_up(state, weight, pull, total, left, right, acc):
    n = MEMBERS
    over_last = (((1,), (1,)), ((), ()))
    eye = lax.broadcasted_iota(jnp.int32, (n, n), 0) == lax.broadcasted_iota(jnp.int32, (n, n), 1)
    away = (eye.astype(F32) - 1.0 / n).astype(BF16)
    away = jnp.concatenate([away, away], axis=1)
    share = jnp.full((8, 2 * n), 1.0 / n, BF16)
    acc[...] = jnp.zeros_like(acc)

    def body(x, carry):
        both = jnp.concatenate([state[0, 2, x], state[1, 2, x]], axis=1)
        z = lax.dot_general(both, away, over_last, preferred_element_type=F32)
        zt = lax.dot_general(away, both, over_last, preferred_element_type=F32)
        mean = lax.dot_general(share, both, over_last, preferred_element_type=F32)[0:1]
        w = weight[pl.ds(x, 1), :]
        y = zt * w
        y_high = y.astype(BF16)
        z_high = z.astype(BF16)
        left[0, x] = y_high
        left[1, x] = (y - y_high.astype(F32)).astype(BF16)
        right[x, :, 0:n] = z_high
        right[x, :, n:2 * n] = (z - z_high.astype(F32)).astype(BF16)
        acc[...] += zt * (pull[pl.ds(x, 1), :] - mean * w)
        return carry

    lax.fori_loop(0, ROWS, body, 0, unroll=8)

    def multiply(x, part):
        a = jnp.concatenate([left[0, 2 * x], left[0, 2 * x + 1]], axis=1)
        b = jnp.concatenate([left[1, 2 * x], left[1, 2 * x + 1]], axis=1)
        z = right[pl.ds(2 * x, 2)].reshape(2 * COLS, 2 * n)
        main = jnp.dot(a, z, preferred_element_type=F32)
        low = jnp.dot(b, z[:, 0:n], preferred_element_type=F32)
        return part + (main[:, 0:n] + (main[:, n:2 * n] + low))

    total[0:n, :] = lax.fori_loop(0, ROWS // 2, multiply, jnp.zeros((n, n), F32), unroll=8)
    total[n:n + 8, :] = jnp.broadcast_to(jnp.sum(acc[...].T, axis=0, keepdims=True), (8, n))


def forecast(*operands):
    plane = (LAYERS, WIDE_ROWS, POSITIONS, SEGMENTS, MEMBERS)
    padded = (LAYERS, WIDE_ROWS, POSITIONS + 2, SEGMENTS, MEMBERS)
    anywhere = pl.BlockSpec(memory_space=pl.ANY)
    vmem = pl.BlockSpec(memory_space=pltpu.VMEM)
    return pl.pallas_call(
        forecast_kernel,
        in_specs=[anywhere] * 7 + [vmem, pl.BlockSpec(memory_space=pltpu.SMEM), vmem, vmem, vmem],
        out_specs=[anywhere, vmem],
        out_shape=[
            jax.ShapeDtypeStruct((LAYERS, 3, ROWS, COLS, MEMBERS), BF16),
            jax.ShapeDtypeStruct((MEMBERS + 8, MEMBERS), F32),
        ],
        scratch_shapes=[
            pltpu.VMEM((LAYERS, 3, WIDE_ROWS, COLS, MEMBERS), BF16),
            pltpu.VMEM((2, LAYERS, 3, WIDE_ROWS // 2, 16, MEMBERS), BF16),
            pltpu.VMEM((LAYERS, 3) + plane[1:], BF16),
            pltpu.VMEM(plane, BF16),
            pltpu.VMEM(padded, BF16),
            pltpu.VMEM(padded, BF16),
            pltpu.VMEM((16 * LINE, MEMBERS), F32),
            pltpu.VMEM((2, ROWS, MEMBERS, COLS), BF16),
            pltpu.VMEM((ROWS, COLS, 2 * MEMBERS), BF16),
            pltpu.VMEM((MEMBERS, COLS), F32),
            pltpu.SemaphoreType.DMA((60,)),
        ],
        compiler_params=params(44),
        cost_estimate=COST,
        name="forecast",
    )(*operands)


def analysis_kernel(state, mix, out, planes):
    pitch = ROWS + 1
    over_last = (((1,), (1,)), ((), ()))
    both = mix[...]

    def body(x, carry):
        s = state[0, 0, pl.ds(2 * x, 2)].reshape(2 * COLS, MEMBERS)
        mixed = lax.dot_general(
            both, jnp.concatenate([s, s], axis=1), over_last, preferred_element_type=F32
        )
        planes[pl.ds(2 * x, MEMBERS, stride=pitch), :] = mixed[:, :COLS]
        planes[pl.ds(2 * x + 1, MEMBERS, stride=pitch), :] = mixed[:, COLS:]
        return carry

    lax.fori_loop(0, ROWS // 2, body, 0, unroll=16)

    def gather(m, carry):
        for k in range(4):
            out[0, 0, 4 * m + k] = planes[pl.ds((4 * m + k) * pitch, ROWS), :].astype(BF16)
        return carry

    lax.fori_loop(0, MEMBERS // 4, gather, 0, unroll=16)


def analyse(state, mix):
    return pl.pallas_call(
        analysis_kernel,
        grid=(LAYERS, 3),
        in_specs=[
            pl.BlockSpec((1, 1, ROWS, COLS, MEMBERS), lambda i, j: (i, j, 0, 0, 0)),
            pl.BlockSpec((MEMBERS, 2 * MEMBERS), lambda i, j: (0, 0)),
        ],
        out_specs=pl.BlockSpec((1, 1, MEMBERS, ROWS, COLS), lambda i, j: (i, j, 0, 0, 0)),
        out_shape=jax.ShapeDtypeStruct((LAYERS, 3, MEMBERS, ROWS, COLS), BF16),
        scratch_shapes=[pltpu.VMEM((MEMBERS * (ROWS + 1), COLS), F32)],
        compiler_params=params(14),
        cost_estimate=COST,
        name="analysis",
    )(state, mix)


def split3(x):
    a = lax.reduce_precision(x, 8, 7)
    b = lax.reduce_precision(x - a, 8, 7)
    c = lax.reduce_precision(x - a - b, 8, 7)
    return [p.astype(BF16) for p in (a, b, c)]


def observed_cells(dest, cell, value, sigma, with_last):
    tiles = lax.axis_size("gy")
    inverse = 1.0 / sigma
    weight = inverse * inverse
    pieces = jnp.stack(split3(weight) + split3(value * weight), 0).reshape(6, -1)
    row = ((dest ^ lax.axis_index("gy"))[:, None] * ROWS + cell // COLS).reshape(-1)
    col = (cell % COLS).reshape(-1)
    row_hot = (row[None, :] == jnp.arange(tiles * ROWS, dtype=jnp.int32)[:, None]).astype(BF16)
    col_hot = col[:, None] == jnp.arange(COLS, dtype=jnp.int32)[None, :]
    spread = jnp.where(col_hot[None], pieces[:, :, None], jnp.zeros((), BF16))
    field = jnp.einsum("rk,pkc->prc", row_hot, spread, preferred_element_type=F32)
    field = jnp.stack([field[2] + field[1] + field[0], field[5] + field[4] + field[3]], 0)
    field = field.reshape(2, tiles, ROWS, COLS).transpose(1, 0, 2, 3)
    bit = tiles // 2
    while bit:
        if bit == 1:
            field, with_last = lax.optimization_barrier((field, with_last))
        swap = [(i, i ^ bit) for i in range(tiles)]
        field = field[:bit] + lax.ppermute(field[bit:], "gy", swap)
        bit //= 2
    return field[0, 0], field[0, 1], with_last


def sum_everywhere(x):
    def other(axis, k):
        return lax.ppermute(x, axis, [(i, i ^ k) for i in range(lax.axis_size(axis))])

    x = x + other("gy", 1)
    for axis, unit in (("gy", 2), ("gx", 1), ("gx", 4)):
        x = (x + other(axis, unit)) + (other(axis, 2 * unit) + other(axis, 3 * unit))
    return x


def transform_kernel(total, mix, work, inverse):
    n = MEMBERS
    full = lax.Precision.HIGHEST
    rows_i = lax.broadcasted_iota(jnp.int32, (n, n), 0)
    cols_i = lax.broadcasted_iota(jnp.int32, (n, n), 1)
    eye = (rows_i == cols_i).astype(F32)
    work[:, 0:n] = total[0:n, :] + F32(n - 1) * eye
    work[:, n:2 * n] = eye
    sub = lax.broadcasted_iota(jnp.int32, (PANEL, n), 0)
    for first in range(0, n, PANEL):
        rows = slice(first, first + PANEL)
        up, inv = work[rows, 0:n], work[rows, n:2 * n]
        cols = [jnp.broadcast_to(up[:, first + k:first + k + 1], (PANEL, n)) for k in range(PANEL)]
        scale = jnp.zeros((PANEL, n), F32)
        for k in range(PANEL):
            pivot = cols[k][k:k + 1]
            scale = jnp.where(sub == k, pivot, scale)
            if k + 1 < PANEL:
                times = jnp.where(sub > k, cols[k], 0.0) * (1.0 / pivot)
                for q in range(k + 1, PANEL):
                    cols[q] = cols[q] - times * cols[q][k:k + 1]
                up = up - times * up[k:k + 1]
                inv = inv - times * inv[k:k + 1]
        scale = lax.rsqrt(scale)
        up, inv = up * scale, inv * scale
        inverse[rows, :] = inv
        after = first + PANEL
        if after < n:
            update = lax.dot_general(
                up, jnp.concatenate([up, inv], axis=1), (((0,), (0,)), ((), ())),
                precision=full, preferred_element_type=F32,
            )
            work[after:, :] = work[after:, :] - update[after:, :]
    low = inverse[...]
    proj = total[n:n + 8, :]
    inner = lax.dot_general(proj, low, (((1,), (1,)), ((), ())), precision=full, preferred_element_type=F32)
    weights = jnp.dot(inner, low, precision=full, preferred_element_type=F32)
    transform_t = weights[0:1] + F32((n - 1) ** 0.5) * low
    spare = (1.0 - jnp.sum(transform_t, axis=1, keepdims=True)) * (1.0 / n)
    value = transform_t + spare
    high = value.astype(BF16)
    mix[:, 0:n] = high
    mix[:, n:2 * n] = (value - high.astype(F32)).astype(BF16)


def make_mix(total):
    vmem = pl.BlockSpec(memory_space=pltpu.VMEM)
    return pl.pallas_call(
        transform_kernel,
        in_specs=[vmem],
        out_specs=vmem,
        out_shape=jax.ShapeDtypeStruct((MEMBERS, 2 * MEMBERS), BF16),
        scratch_shapes=[
            pltpu.VMEM((MEMBERS, 2 * MEMBERS), F32),
            pltpu.VMEM((MEMBERS, MEMBERS), F32),
        ],
        compiler_params=params(8),
        cost_estimate=COST,
        name="transform",
    )(total)


def on_device(ensemble, layer_depth, obs_dest, obs_cell, obs_value, obs_sigma):
    row0 = lax.axis_index("gx") * ROWS - HALO + jnp.arange(WIDE_ROWS, dtype=jnp.int32)
    col0 = lax.axis_index("gy") * COLS - HALO + jnp.arange(COLS + 2 * HALO, dtype=jnp.int32)
    row_in = (row0 >= 0) & (row0 < lax.axis_size("gx") * ROWS)
    col_in = (col0 >= 0) & (col0 < lax.axis_size("gy") * COLS)
    d = layer_depth
    d = jnp.concatenate(
        [shift(d[:, ROWS - HALO:], "gx", 1), d, shift(d[:, :HALO], "gx", -1)], axis=1
    )
    own, left_out, right_out, north, south = all_rows(ensemble)
    observed = (obs_dest[0, 0], obs_cell[0, 0], obs_value[0, 0], obs_sigma[0, 0])
    d, north, south = lax.optimization_barrier((d, north, south))
    top = shift(south, "gx", 1)
    bottom = shift(north, "gx", -1)
    left = shift(right_out, "gy", 1)
    right = shift(left_out, "gy", -1)
    d, left, observed = lax.optimization_barrier((d, left, observed))
    d = jnp.concatenate(
        [shift(d[:, :, COLS - HALO:], "gy", 1), d, shift(d[:, :, :HALO], "gy", -1)], axis=2
    )
    d = jnp.where(row_in[:, None] & col_in[None, :], (HALF * HALF) * d, 0.0).astype(BF16)
    d = d.reshape(LAYERS, WIDE_ROWS, SEGMENTS, POSITIONS).transpose(0, 1, 3, 2)
    depth = jnp.broadcast_to(d[..., None], d.shape + (MEMBERS,))
    mask = col_in.reshape(SEGMENTS, POSITIONS).T.astype(BF16)
    mask = jnp.stack([jnp.zeros_like(mask), mask], axis=0)
    masks = jnp.broadcast_to(mask[..., None], mask.shape + (MEMBERS,))
    row_in = row_in.astype(jnp.int32)[None, :]
    sides = jnp.stack([left, right], axis=0)
    corner_t = shift(sides[:, :, :, 12:], "gx", 1)
    corner_b = shift(sides[:, :, :, :4], "gx", -1)

    weight, pull, (depth, masks) = observed_cells(*observed, (depth, masks))
    state, total = forecast(
        own, top, bottom, left, right, corner_t, corner_b, depth, row_in, masks, weight, pull
    )
    total = sum_everywhere(total)
    return analyse(state, make_mix(total))


def solution(mesh):
    in_specs = (
        P(None, None, None, "gx", "gy"),
        P(None, "gx", "gy"),
        P("gx", "gy", None),
        P("gx", "gy", None, None),
        P("gx", "gy", None, None),
        P("gx", "gy", None, None),
    )
    out_specs = P(None, None, None, "gx", "gy")
    return jax.shard_map(
        on_device, mesh=mesh, in_specs=in_specs, out_specs=out_specs, check_vma=False
    )
```
